128 devices in a mesh: pool: 8 (over z, y_hi), seq: 16 (over x, y_lo, core).
Axes of the slice: x: 4, y: 4 (y_hi: 2, y_lo: 2; y = y_hi * 2 + y_lo), z: 4, core: 2. Of those that a mesh axis runs over, the one named last changes fastest.
Arguments:
- patches: bfloat16 [8192, 1280], P(('pool', 'seq')), may hold values from -6 to 6
- merge_up: bfloat16 [5120, 5120], P(None, 'seq'), may hold values from -0.078125 to 0.078125
- merge_down: bfloat16 [5120, 8192], P('seq'), may hold values from -0.078125 to 0.078125
- image_pos: int32 [2048], P(('pool', 'seq')), may hold values from 0 to 6143, as said below
- text_rows: bfloat16 [6144, 8192], P('seq'), may hold values from -6 to 6
- segment: int32 [6144], P('seq'), may hold values from 0 to 3, never falling along the last dimension, each value on 1 to 4608 neighbouring positions
- query_weight: bfloat16 [8192, 8192], P('seq', 'pool')
- key_weight: bfloat16 [8192, 1024], P('seq', 'pool')
- value_weight: bfloat16 [8192, 1024], P('seq', 'pool'), may hold values from -0.0625 to 0.0625
Outputs:
- attended: bfloat16 [6144, 8192], P('seq', 'pool')
The draws below stay inside these ranges and needn't reach their ends.
Inputs may be any that keep to these rules, and one draw needn't show every extreme that they name: `image_pos`: positions are all distinct. Of the 16 image tokens of one device, at most 2 lie in one block of 384 positions, and in every device's tokens some block holds exactly 2. `segment`: request numbers never fall along the sequence.
All inputs are finite; a program needn't handle non-finite values.
Results may differ from the reference program's by a relative error of at most 0.02.
The reference program's roundings to bfloat16 on the way count: a program that leaves them out, or rounds other values in their place, can miss the bound.
Values may be sent and summed in bfloat16 or wider, within the bound.
No kernel may reach another device: no remote copies, remote signals or barrier semaphores. Data moves between devices by JAX's collectives and lax.ppermute only.
A program may use at most 128 MiB of HBM per device.

```python
import math
import jax
import jax.numpy as jnp
import numpy as np
from jax import lax

D = 8192
VW = 1280
HEADS = 64
KV_HEADS = 8
HD = 128
TOK_DEV = 384
PATCH_DEV = 64
MW = 5120
NPATCH = 8192
IMG_TOK = 2048
SEQLEN = 6144
N_POOL = 8
N_SEQ = 16


def shared_query(key):
    return jax.random.normal(key, (D, HEADS * HD), jnp.float32) / math.sqrt(D)


def draw_query_weight(key, part):
    base = shared_query(key)
    return base.astype(jnp.bfloat16)


def draw_key_weight(key, part):
    key = jax.random.fold_in(key, 12)
    fresh_key = jax.random.fold_in(key, 0)
    fresh = jax.random.normal(fresh_key, (D, KV_HEADS * HD), jnp.float32) / math.sqrt(D)
    return (2.0 * fresh).astype(jnp.bfloat16)


def draw_image_pos(key, part):
    key = jax.random.fold_in(key, 5)
    device_count = N_POOL * N_SEQ
    own_rows = PATCH_DEV // 4
    first_key, second_key, third_key = jax.random.split(key, 3)
    shard_order = jax.vmap(lambda subkey: jax.random.permutation(subkey, N_SEQ))(jax.random.split(first_key, device_count))
    slot_order = jax.vmap(lambda subkey: jax.random.permutation(subkey, 2 * N_SEQ - 2))(jax.random.split(second_key, device_count))
    slot_order = slot_order[:, :own_rows - 2]
    leading = shard_order[:, :1]
    remaining = jnp.take_along_axis(shard_order, 1 + slot_order // 2, axis=1)
    shard_of = jnp.concatenate([leading, leading, remaining], axis=1).reshape(-1).astype(jnp.int32)
    matches = (shard_of[:, None] == jnp.arange(N_SEQ, dtype=jnp.int32)[None, :]).astype(jnp.int32)
    slot_rank = jnp.sum((jnp.cumsum(matches, axis=0) - matches) * matches, axis=1)
    offsets = jax.vmap(lambda subkey: jax.random.permutation(subkey, TOK_DEV))(jax.random.split(third_key, N_SEQ)).astype(jnp.int32)
    return (shard_of * TOK_DEV + offsets[shard_of, slot_rank]).astype(jnp.int32)


def levels(rng, extent, shards, low, largest):
    loudness = 1.0
    for position, parts in shards:
        heights = jax.random.uniform(jax.random.fold_in(jax.random.fold_in(rng, 6), position), (parts,), jnp.float32, low / len(shards), largest / len(shards))
        loudness = loudness * jnp.repeat(jnp.exp(heights), extent[position] // parts).reshape((-1,) + (1,) * (len(extent) - 1 - position))
    return loudness


def profile(number_of, total, limit, slope):
    portions = [(1 << 20) // math.isqrt(standing ** slope) + 1 for standing in range(2, number_of + 1)]
    surplus, holding = total - limit - (number_of - 1), [1] * (number_of - 1)
    while surplus > 0:
        movable = [i for i in range(number_of - 1) if holding[i] < limit]
        whole, left = sum([portions[i] for i in movable]), surplus
        for i in movable:
            addition = min(limit - holding[i], max(1, left * portions[i] // whole), surplus)
            holding[i] = holding[i] + addition
            surplus = surplus - addition
    return np.array([limit] + holding)


def ragged(own_key, number_of, total, most, slope):
    if number_of == 2:
        one = jax.random.randint(own_key, (), max(1, total - most), min(most, total - 1) + 1)
        return jnp.stack([one, total - one])
    sizes = jnp.asarray(profile(number_of, total, most, slope), jnp.int32)
    couples = (number_of - 1) // 2
    source_of, sink = sizes[1:1 + 2 * couples:2], sizes[2:2 + 2 * couples:2]
    slack = jnp.minimum(source_of - 1, most - sink)
    passed = jax.random.randint(jax.random.fold_in(own_key, 1), (couples,), 0, 1 << 20) % (slack + 1)
    sizes = sizes.at[1:1 + 2 * couples:2].set(source_of - passed).at[2:2 + 2 * couples:2].set(sink + passed)
    return sizes[jax.random.permutation(jax.random.fold_in(own_key, 2), number_of)]


def normal_values(key, extent, width, limit, pieces=(), held_as=jnp.bfloat16):
    values = jax.random.normal(key, extent, jnp.float32) * width
    if len(pieces) > 0:
        values = levels(key, extent, pieces, -0.22, 0.18) * values
    return jnp.clip(values, min=-limit, max=limit).astype(held_as)


def setup_inputs(seed: int = 0) -> dict:
    streams_of = jax.random.split(jax.random.key(seed), 10)
    patches = normal_values(streams_of[0], (NPATCH, VW), 1.0, 6.0, ((0, 128),))
    merge_up = normal_values(streams_of[1], (MW, MW), MW ** -0.5, 0.078125, ((1, 16),))
    merge_down = normal_values(streams_of[2], (MW, D), MW ** -0.5, 0.078125, ((0, 16),))
    image_pos = draw_image_pos(jax.random.fold_in(streams_of[9], 71), 0)
    text_rows = normal_values(streams_of[4], (SEQLEN, D), 1.0, 6.0, ((0, 16),))
    segment = jnp.searchsorted(jnp.cumsum(ragged(streams_of[5], 4, SEQLEN, SEQLEN * 3 // 4, 0)), jnp.arange(SEQLEN), side="right").astype(jnp.int32)
    query_weight = draw_query_weight(jax.random.fold_in(streams_of[9], 71), 0)
    key_weight = draw_key_weight(jax.random.fold_in(streams_of[9], 71), 0)
    value_weight = normal_values(streams_of[8], (D, KV_HEADS * HD), D ** -0.5, 0.0625, ((0, 16), (1, 8)))
    return {"patches": patches, "merge_up": merge_up, "merge_down": merge_down, "image_pos": image_pos, "text_rows": text_rows, "segment": segment, "query_weight": query_weight, "key_weight": key_weight, "value_weight": value_weight}


NORM_EPS = 1e-06
ROPE_BASE = 1000000.0

def rms_rows(matrix):
    return matrix * lax.rsqrt(lax.optimization_barrier(jnp.mean(matrix * matrix, axis=-1, keepdims=True)) + NORM_EPS)

def rotate(tensor, positions):
    half_width = tensor.shape[-1] // 2
    frequency = ROPE_BASE ** (-(jnp.arange(half_width, dtype=jnp.float32) * 2.0 / tensor.shape[-1]))
    angles = positions.astype(jnp.float32)[:, None] * frequency[None, :]
    cosine = jnp.cos(angles)[:, None, :]
    sine_part = jnp.sin(angles)[:, None, :]
    first = tensor[..., :half_width]
    second = tensor[..., half_width:]
    return jnp.concatenate([first * cosine - second * sine_part, second * cosine + first * sine_part], axis=-1)

def reference(patches, merge_up, merge_down, image_pos, text_rows, segment, query_weight, key_weight, value_weight):
    normed = rms_rows(patches.astype(jnp.float32)).astype(jnp.bfloat16)
    merged = normed.reshape(IMG_TOK, MW)
    hidden = jax.nn.gelu(jnp.dot(merged, merge_up, preferred_element_type=jnp.float32), approximate=False).astype(jnp.bfloat16)
    image_rows = jnp.dot(hidden, merge_down, preferred_element_type=jnp.float32).astype(jnp.bfloat16)
    seq_rows = text_rows.at[image_pos].set(image_rows)
    xnorm = rms_rows(seq_rows.astype(jnp.float32)).astype(jnp.bfloat16)
    positions = jnp.arange(SEQLEN, dtype=jnp.int32)
    queries = rotate(jnp.dot(xnorm, query_weight, preferred_element_type=jnp.float32).reshape(SEQLEN, HEADS, HD), positions).astype(jnp.bfloat16)
    key_rows = rotate(jnp.dot(xnorm, key_weight, preferred_element_type=jnp.float32).reshape(SEQLEN, KV_HEADS, HD), positions).astype(jnp.bfloat16)
    values = jnp.dot(xnorm, value_weight, preferred_element_type=jnp.float32).astype(jnp.bfloat16).reshape(SEQLEN, KV_HEADS, HD)
    group_size = HEADS // KV_HEADS
    queries = queries.reshape(SEQLEN // 512, 512, KV_HEADS, group_size, HD)
    score_scale = HD ** (-0.5)

    def one_block(block_index):
        query_block = queries[block_index]
        query_positions = block_index * 512 + jnp.arange(512, dtype=jnp.int32)
        query_segment = lax.dynamic_slice_in_dim(segment, (block_index * 512).astype(jnp.int32), 512)
        allowed = (positions[None, :] <= query_positions[:, None]) & (segment[None, :] == query_segment[:, None])

        def one_head(kv_head):
            query_head = query_block[:, kv_head].astype(jnp.float32)
            key_head = key_rows[:, kv_head].astype(jnp.float32)
            scores = jnp.einsum('tgd,sd->gts', query_head, key_head) * score_scale
            scores = jnp.where(allowed[None], scores, -1e+30)
            row_max = lax.optimization_barrier(jnp.max(scores, axis=-1, keepdims=True))
            weights = jnp.where(allowed[None], jnp.exp(scores - row_max), 0.0)
            denominator = lax.optimization_barrier(jnp.sum(weights, axis=-1))
            rounded = lax.optimization_barrier(weights.astype(jnp.bfloat16))
            mixed = jnp.einsum('gts,sd->gtd', rounded.astype(jnp.float32), values[:, kv_head].astype(jnp.float32))
            return mixed / denominator[..., None]
        head_outputs = lax.map(one_head, jnp.arange(KV_HEADS, dtype=jnp.int32))
        return head_outputs.transpose(2, 0, 1, 3).reshape(512, HEADS * HD).astype(jnp.bfloat16)
    blocks = lax.map(one_block, jnp.arange(SEQLEN // 512, dtype=jnp.int32))
    return blocks.reshape(SEQLEN, HEADS * HD)
```

```python
import functools

import jax
import jax.numpy as jnp
from jax import lax
from jax.experimental import pallas as pl
from jax.experimental.pallas import tpu as pltpu
from jax.sharding import PartitionSpec as P

HD = 128
CAP = 2
AUX = 128
NORM_EPS = 1e-06
ROPE_BASE = 1000000.0
BIG_NEG = -1e30
VMEM_BYTES = 56 * 1024 * 1024
X, Y, C = 4, 2, 2


def rms_rows(matrix):
    return matrix * lax.rsqrt(jnp.mean(matrix * matrix, axis=-1, keepdims=True) + NORM_EPS)


def seq_shift(array, dx, dy, dc):
    pairs = []
    for source in range(X * Y * C):
        x, y, c = source // (Y * C), source // C % Y, source % C
        pairs.append((source, ((x + dx) % X) * Y * C + (y ^ dy) * C + (c ^ dc)))
    return lax.ppermute(array, "seq", pairs)


OFFSETS = [(dx, dy) for dx in range(X) for dy in range(Y)]


def qkv_kernel(text_ref, slots_ref, weight_ref, cos_ref, sin_ref, out_ref, x_ref):
    rows, width = text_ref.shape
    slot_count = slots_ref.shape[0]
    step = pl.program_id(0)
    chunk = 1024

    @pl.when(step == 0)
    def _():
        aux = slots_ref[:, width:].astype(jnp.float32)
        offset = aux[:, 0:1] * 128.0 + aux[:, 1:2]
        offset = jnp.where(aux[:, 2:3] > 0.5, offset, -1.0).astype(jnp.int32)
        token = lax.broadcasted_iota(jnp.int32, (slot_count, rows), 1)
        select = jnp.where(offset == token, 1.0, 0.0).T.astype(jnp.bfloat16)
        held = jnp.dot(select, slots_ref[:, width:], preferred_element_type=jnp.float32)[:, 2:3] > 0.5
        total = jnp.zeros((rows, 1), jnp.float32)
        for start in range(0, width, chunk):
            part = slice(start, start + chunk)
            image = jnp.dot(select, slots_ref[:, part], preferred_element_type=jnp.float32)
            mixed = jnp.where(held, image, text_ref[:, part].astype(jnp.float32))
            total += jnp.sum(mixed * mixed, axis=1, keepdims=True)
            x_ref[:, part] = mixed.astype(jnp.bfloat16)
        scale = lax.rsqrt(total / width + NORM_EPS)
        for start in range(0, width, chunk):
            part = slice(start, start + chunk)
            x_ref[:, part] = (x_ref[:, part].astype(jnp.float32) * scale).astype(jnp.bfloat16)

    acc = jnp.dot(x_ref[...], weight_ref[...], preferred_element_type=jnp.float32)
    last = pl.num_programs(0) - 1
    cosine, sine = cos_ref[...], sin_ref[...]

    def turned(part):
        return part * cosine + pltpu.roll(part, HD // 2, 1) * sine

    out_ref[:, :HD] = turned(acc[:, :HD]).astype(jnp.bfloat16)

    @pl.when(step < last)
    def _():
        out_ref[:, HD:] = turned(acc[:, HD:]).astype(jnp.bfloat16)

    @pl.when(step == last)
    def _():
        out_ref[:, HD:] = acc[:, HD:].astype(jnp.bfloat16)


def project(text_rows, slots, weights, cosine, sine):
    rows, width = text_rows.shape
    columns = weights.shape[1]
    block = 2 * HD
    whole = lambda shape: pl.BlockSpec(shape, lambda n: (0, 0), pipeline_mode=pl.Buffered(1))
    return pl.pallas_call(
        qkv_kernel,
        grid=(columns // block,),
        in_specs=[
            whole((rows, width)),
            whole(slots.shape),
            pl.BlockSpec((width, block), lambda n: (0, n)),
            whole((rows, HD)),
            whole((rows, HD)),
        ],
        out_specs=pl.BlockSpec((rows, block), lambda n: (0, n)),
        out_shape=jax.ShapeDtypeStruct((rows, columns), jnp.bfloat16),
        scratch_shapes=[pltpu.VMEM((rows, width), jnp.bfloat16)],
        compiler_params=pltpu.CompilerParams(vmem_limit_bytes=VMEM_BYTES),
        name="project",
    )(text_rows, slots, weights, cosine, sine)


GROUP = 2


def attention_kernel(info_ref, q_ref, kv_ref, start_ref, out_ref, qs_ref, top_ref, sum_ref, acc_ref):
    rows = q_ref.shape[0]
    heads = out_ref.shape[1] // HD
    groups = heads // GROUP
    wide = GROUP * rows
    me = info_ref[0]
    first = info_ref[1]
    edge = info_ref[2]
    factor = HD ** (-0.5) * 1.4426950408889634
    for h in range(heads):
        qs_ref[h * rows:(h + 1) * rows, :] = q_ref[:, h * HD:(h + 1) * HD]

    def block(index, masked, fresh):
        keys = kv_ref[index, :, :HD]
        values = kv_ref[index, :, HD:]
        if masked:
            key_at = index * rows + lax.broadcasted_iota(jnp.int32, (rows, rows), 0)
            query_at = me * rows + lax.broadcasted_iota(jnp.int32, (rows, rows), 1)
            allowed = (key_at <= query_at) & (key_at >= start_ref[0:1, :])
            allowed = jnp.concatenate([allowed] * GROUP, axis=1)
        for g in range(groups):
            part = slice(g * wide, (g + 1) * wide)
            scores = lax.dot_general(
                keys, qs_ref[part, :], (((1,), (1,)), ((), ())), preferred_element_type=jnp.float32
            )
            if masked:
                scores = jnp.where(allowed, scores, BIG_NEG)
            top = jnp.max(scores, axis=0, keepdims=True)
            if not fresh:
                old = top_ref[:, part]
                top = jnp.maximum(old, top)
            probs = jnp.exp2((scores - top) * factor)
            total = jnp.sum(probs, axis=0, keepdims=True)
            mixed = lax.dot_general(
                values, probs.astype(jnp.bfloat16), (((0,), (0,)), ((), ())), preferred_element_type=jnp.float32
            )
            if not fresh:
                shrink = jnp.exp2((old - top) * factor)
                total += sum_ref[:, part] * shrink
                mixed += acc_ref[:, part] * shrink
            top_ref[:, part] = top
            sum_ref[:, part] = total
            acc_ref[:, part] = mixed

    block(me, True, True)

    def step(i, _):
        index = me - 1 - i
        needs = index * rows < edge

        @pl.when(needs)
        def _():
            block(index, True, False)

        @pl.when(jnp.logical_not(needs))
        def _():
            block(index, False, False)

        return 0

    lax.fori_loop(0, me - first, step, 0)
    for h in range(heads):
        part = slice(h * rows, (h + 1) * rows)
        out_ref[:, h * HD:(h + 1) * HD] = (acc_ref[:, part] / sum_ref[:, part]).T.astype(jnp.bfloat16)


def attend(info, qkv, kv_all, starts, heads):
    rows = qkv.shape[0]
    vmem = pl.BlockSpec(memory_space=pltpu.VMEM)
    return pl.pallas_call(
        attention_kernel,
        in_specs=[pl.BlockSpec(memory_space=pltpu.SMEM), vmem, vmem, vmem],
        out_specs=vmem,
        out_shape=jax.ShapeDtypeStruct((rows, heads * HD), jnp.bfloat16),
        scratch_shapes=[
            pltpu.VMEM((heads * rows, HD), jnp.bfloat16),
            pltpu.VMEM((1, heads * rows), jnp.float32),
            pltpu.VMEM((1, heads * rows), jnp.float32),
            pltpu.VMEM((HD, heads * rows), jnp.float32),
        ],
        compiler_params=pltpu.CompilerParams(vmem_limit_bytes=VMEM_BYTES),
        name="attend",
    )(info, qkv, kv_all, starts)


def per_device(
    patches,
    merge_up,
    merge_down,
    image_pos,
    text_rows,
    segment,
    query_weight,
    key_weight,
    value_weight,
):
    seq_count = lax.axis_size("seq")
    seq_index = lax.axis_index("seq")
    rows, width = text_rows.shape
    bf16, f32 = jnp.bfloat16, jnp.float32

    with jax.named_scope("weights"):
        weights = lax.all_gather(
            jnp.concatenate([query_weight, key_weight, value_weight], axis=1), "seq", axis=0, tiled=True
        )

    with jax.named_scope("merger_up"):
        normed = rms_rows(patches.astype(f32)).astype(bf16)
        merged = normed.reshape(-1, 4 * patches.shape[1])
        own, merged_width = merged.shape
        below = jnp.sum((segment[None, :] < jnp.arange(1, 4, dtype=jnp.int32)[:, None]).astype(jnp.int32), axis=1)
        counts = jnp.concatenate([below // 128, below % 128]).astype(bf16)
        counts = jnp.broadcast_to(jnp.pad(counts, (0, AUX - 6))[None, :], (own, AUX))
        merged = jnp.concatenate([merged, counts], axis=1)
        pieces = [merged if (dx, dy) == (0, 0) else seq_shift(merged, dx, dy, 0) for dx, dy in OFFSETS]
        mine = jnp.concatenate(pieces, axis=0)
        other = seq_shift(mine, 0, 0, 1)

        def up(block):
            return jax.nn.gelu(
                jnp.dot(block[:, :merged_width], merge_up, preferred_element_type=f32), approximate=False
            ).astype(bf16)

        counted = jnp.sum(
            mine[::own, merged_width:].astype(f32) + other[::own, merged_width:].astype(f32), axis=0
        )
        ends = (counted[:3] * 128.0 + counted[3:6]).astype(jnp.int32)
        hidden_other = up(other)
        hidden_mine = up(mine)

    with jax.named_scope("merger_down"):
        partial_other = jnp.dot(hidden_other, merge_down, preferred_element_type=f32).astype(bf16)
        received = seq_shift(partial_other, 0, 0, 1)
        partial = jnp.dot(hidden_mine, merge_down, preferred_element_type=f32) + received.astype(f32)
        partial = partial.reshape(X, Y * own, width)
        received = [seq_shift(partial[dx].astype(bf16), -dx, 0, 0) for dx in range(1, X)]
        partial = partial[0] + sum(piece.astype(f32) for piece in received)
        received = seq_shift(partial[own:].astype(bf16), 0, 1, 0)
        image_rows = (partial[:own] + received.astype(f32)).astype(bf16)

    with jax.named_scope("route"):
        target = image_pos // rows
        offset = image_pos % rows
        matches = (target[:, None] == jnp.arange(seq_count, dtype=jnp.int32)[None, :]).astype(jnp.int32)
        slot_rank = jnp.sum((jnp.cumsum(matches, axis=0) - matches) * matches, axis=1)
        slot_index = target * CAP + slot_rank
        select = (slot_index[None, :] == jnp.arange(seq_count * CAP, dtype=jnp.int32)[:, None]).astype(bf16)
        marks = jnp.stack([offset // 128, offset % 128, jnp.ones_like(offset)], axis=1).astype(bf16)
        marks = jnp.pad(marks, ((0, 0), (0, AUX - 3)))
        send = jnp.dot(
            select, jnp.concatenate([image_rows, marks], axis=1), preferred_element_type=f32
        ).astype(bf16)
        got = lax.all_to_all(
            send.reshape(seq_count, CAP, width + AUX), "seq", split_axis=0, concat_axis=0, tiled=True
        )
        slots = lax.all_gather(got, "pool", axis=0, tiled=True).reshape(-1, width + AUX)

    with jax.named_scope("project"):
        positions = (seq_index * rows + jnp.arange(rows, dtype=jnp.int32)).astype(f32)
        half = HD // 2
        frequency = ROPE_BASE ** (-(jnp.arange(half, dtype=f32) * 2.0 / HD))
        angles = positions[:, None] * frequency[None, :]
        cosine, sine = jnp.cos(angles), jnp.sin(angles)
        qkv = project(
            text_rows,
            slots,
            weights,
            jnp.concatenate([cosine, cosine], axis=1),
            jnp.concatenate([-sine, sine], axis=1),
        )
        q_columns = query_weight.shape[1]
        kv_all = lax.all_gather(qkv[:, q_columns:], "seq", axis=0, tiled=True)

    with jax.named_scope("attend"):
        before = jnp.concatenate([jnp.zeros((1,), jnp.int32), ends])
        starts = jnp.sum(
            jnp.where(segment[None, :] == jnp.arange(4, dtype=jnp.int32)[:, None], before[:, None], 0), axis=0
        )
        info = jnp.stack([seq_index, starts[0] // rows, starts[-1]]).astype(jnp.int32)
        return attend(
            info,
            qkv,
            kv_all.reshape(seq_count, rows, 2 * HD),
            starts[None, :],
            q_columns // HD,
        )


def solution(mesh):
    return jax.shard_map(
        per_device,
        mesh=mesh,
        in_specs=(
            P(("pool", "seq"), None),
            P(None, "seq"),
            P("seq", None),
            P(("pool", "seq")),
            P("seq", None),
            P("seq"),
            P("seq", "pool"),
            P("seq", "pool"),
            P("seq", "pool"),
        ),
        out_specs=P("seq", "pool"),
        check_vma=False,
    )
```

```python
import jax
import jax.numpy as jnp
from jax import lax
from jax.experimental import pallas as pl
from jax.experimental.pallas import tpu as pltpu
from jax.sharding import PartitionSpec as P

HD = 128
CAP = 2
AUX = 128
NORM_EPS = 1e-06
ROPE_BASE = 1000000.0
BIG_NEG = -1e30
LOG2E = 1.4426950408889634
VMEM_BYTES = 56 * 1024 * 1024
X, Y, C = 4, 2, 2
Z, YH = 4, 2
CHUNK = 1024


def rms_rows(matrix):
    return matrix * lax.rsqrt(jnp.mean(matrix * matrix, axis=-1, keepdims=True) + NORM_EPS)


def seq_shift(array, dx, dy, dc):
    pairs = []
    for source in range(X * Y * C):
        x, y, c = source // (Y * C), source // C % Y, source % C
        pairs.append((source, ((x + dx) % X) * Y * C + (y ^ dy) * C + (c ^ dc)))
    return lax.ppermute(array, "seq", pairs)


HALF_D = 4096


def pool_shift(array, dz, dy):
    pairs = []
    for source in range(Z * YH):
        z, y = source // YH, source % YH
        pairs.append((source, ((z + dz) % Z) * YH + (y ^ dy)))
    return lax.ppermute(array, "pool", pairs)


def whole(shape):
    return pl.BlockSpec(shape, lambda n: (0, 0), pipeline_mode=pl.Buffered(1))


def patch_kernel(patches_ref, segment_ref, out_ref):
    own = out_ref.shape[0]
    patch_count, width = patches_ref.shape
    normed = rms_rows(patches_ref[...].astype(jnp.float32)).astype(jnp.bfloat16)
    token = lax.broadcasted_iota(jnp.int32, (own, patch_count), 0)
    patch = lax.broadcasted_iota(jnp.int32, (own, patch_count), 1)
    for k in range(4):
        pick = jnp.where(patch == 4 * token + k, 1.0, 0.0).astype(jnp.bfloat16)
        out_ref[:, k * width:(k + 1) * width] = jnp.dot(
            pick, normed, preferred_element_type=jnp.float32
        ).astype(jnp.bfloat16)
    lane = lax.broadcasted_iota(jnp.int32, (own, AUX), 1)
    marks = jnp.zeros((own, AUX), jnp.float32)
    for v in range(1, 4):
        before = jnp.sum(jnp.where(segment_ref[...] < v, 1.0, 0.0), axis=1, keepdims=True)
        high = jnp.floor(before * (1.0 / 128.0))
        marks += jnp.where(lane == v - 1, high, 0.0) + jnp.where(lane == v + 2, before - 128.0 * high, 0.0)
    out_ref[:, 4 * width:] = marks.astype(jnp.bfloat16)


def prepare(patches, segment):
    vmem = pl.BlockSpec(memory_space=pltpu.VMEM)
    return pl.pallas_call(
        patch_kernel,
        in_specs=[vmem, vmem],
        out_specs=vmem,
        out_shape=jax.ShapeDtypeStruct((patches.shape[0] // 4, 4 * patches.shape[1] + AUX), jnp.bfloat16),
        name="prepare",
    )(patches, segment[None, :])


def merger_kernel(*refs):
    pieces, (up_a, up_b, down_a, down_b), outs = refs[:X], refs[X:X + 4], refs[X + 4:X + 4 + X + Y]
    hidden_ref = refs[-1]
    rows = pieces[0].shape[0]
    units = up_a.shape[1]
    depth = up_a.shape[0]
    step = pl.program_id(0)
    half = pl.num_programs(0) // 2

    @pl.when(step == 0)
    def _():
        merged = jnp.concatenate([piece[:, :depth] for piece in pieces], axis=0)
        for at, up in ((0, up_a), (1, up_b)):
            value = jnp.dot(merged, up[...], preferred_element_type=jnp.float32)
            value = 0.5 * value * (1.0 + lax.erf(value * (0.5 ** 0.5)))
            hidden_ref[at] = value.astype(jnp.bfloat16)

    total = jnp.dot(hidden_ref[0], down_a[...], preferred_element_type=jnp.float32)
    total += jnp.dot(hidden_ref[1], down_b[...], preferred_element_type=jnp.float32)

    @pl.when(step < half)
    def _():
        for dx in range(X):
            outs[dx][...] = total[dx * rows:(dx + 1) * rows].astype(outs[dx].dtype)

    @pl.when(step >= half)
    def _():
        own = rows // Y
        for dx in range(X):
            for dy in range(Y):
                at = dx * rows + dy * own
                outs[X + dy][dx * own:(dx + 1) * own, :] = total[at:at + own].astype(outs[X + dy].dtype)


def merger(pieces, ups, downs):
    rows = pieces[0].shape[0]
    depth, units = ups[0].shape
    width = downs[0].shape[1]
    block = 1024
    half = HALF_D // block
    first = lambda shape: pl.BlockSpec(shape, lambda n: (0, jnp.minimum(n, half - 1)))
    second = lambda shape: pl.BlockSpec(shape, lambda n: (0, jnp.maximum(n - half, 0)))
    own = rows // Y
    shape = jax.ShapeDtypeStruct
    return pl.pallas_call(
        merger_kernel,
        grid=(width // block,),
        in_specs=[whole(pieces[0].shape)] * X
        + [whole((depth, units))] * 2
        + [pl.BlockSpec((units, block), lambda n: (0, n))] * 2,
        out_specs=[first((rows, block))] * X + [second((X * own, block))] * Y,
        out_shape=[shape((rows, HALF_D), jnp.float32 if dx == 0 else jnp.bfloat16) for dx in range(X)]
        + [shape((X * own, width - HALF_D), jnp.float32 if dy == 0 else jnp.bfloat16) for dy in range(Y)],
        scratch_shapes=[pltpu.VMEM((2, X * rows, units), jnp.bfloat16)],
        compiler_params=pltpu.CompilerParams(vmem_limit_bytes=VMEM_BYTES),
        name="merger",
    )(*pieces, *ups, *downs)


def turned(part, cosine, sine):
    return part * cosine + pltpu.roll(part, HD // 2, 1) * sine


def place_kernel(
    text_ref, a0, a1, a2, a3, b0, b1, weight_ref, cos_ref, sin_ref,
    x_ref, kv_ref, scale_ref, pick_a, pick_b, held_ref, total_ref, sum_ref,
):
    rows = text_ref.shape[0]
    step = pl.program_id(0)
    steps = pl.num_programs(0)
    half = HALF_D // CHUNK
    cap = a0.shape[0] // YH
    aux_at = b0.shape[1] - AUX

    @pl.when(step == 0)
    def _():
        marks_b = jnp.concatenate([b0[:, aux_at:], b1[:, aux_at:]], axis=0)
        blocks = []
        for dz in range(Z):
            for ref in (b0, b1):
                blocks.append(ref[dz * cap:(dz + 1) * cap, aux_at:])
        marks_a = jnp.concatenate(blocks, axis=0)
        for marks, pick in ((marks_a, pick_a), (marks_b, pick_b)):
            value = marks.astype(jnp.float32)
            offset = value[:, 0:1] * 128.0 + value[:, 1:2]
            offset = jnp.where(value[:, 2:3] > 0.5, offset, -1.0).astype(jnp.int32)
            token = lax.broadcasted_iota(jnp.int32, (value.shape[0], rows), 1)
            pick[...] = jnp.where(offset == token, 1.0, 0.0).T.astype(jnp.bfloat16)
        held_ref[...] = jnp.dot(pick_b[...], marks_b, preferred_element_type=jnp.float32)
        total_ref[...] = jnp.zeros_like(total_ref)
        sum_ref[...] = jnp.zeros_like(sum_ref)

    def add(pick, refs, at):
        part = pl.ds(pl.multiple_of(at * CHUNK, CHUNK), CHUNK)
        slots = jnp.concatenate([ref[:, part] for ref in refs], axis=0)
        image = jnp.dot(pick[...], slots, preferred_element_type=jnp.float32)
        mixed = jnp.where(held_ref[:, 2:3] > 0.5, image, text_ref[...].astype(jnp.float32))
        total_ref[...] += jnp.sum(mixed * mixed, axis=1, keepdims=True)
        rounded = mixed.astype(jnp.bfloat16)
        x_ref[...] = rounded
        sum_ref[...] += jnp.dot(rounded, weight_ref[...], preferred_element_type=jnp.float32)

    @pl.when(step < half)
    def _():
        add(pick_a, (a0, a1, a2, a3), step)

    @pl.when(step >= half)
    def _():
        add(pick_b, (b0, b1), step - half)

    @pl.when(step == steps - 1)
    def _():
        scale = lax.rsqrt(total_ref[:, 0:1] / (steps * CHUNK) + NORM_EPS)
        key = turned(sum_ref[:, :HD] * scale, cos_ref[...], sin_ref[...])
        kv_ref[:, :HD] = key.astype(jnp.bfloat16)
        kv_ref[:, HD:] = (sum_ref[:, HD:] * scale).astype(jnp.bfloat16)
        scale_ref[...] = jnp.broadcast_to(scale, scale_ref.shape)


def place(text_rows, slots_a, slots_b, weights, cosine, sine):
    rows, width = text_rows.shape
    slot_count = X * slots_a[0].shape[0]
    kv_block = weights.shape[1] // (2 * HD) - 1
    shape = jax.ShapeDtypeStruct
    return pl.pallas_call(
        place_kernel,
        grid=(width // CHUNK,),
        in_specs=[pl.BlockSpec((rows, CHUNK), lambda n: (0, n))]
        + [whole(piece.shape) for piece in slots_a]
        + [whole(piece.shape) for piece in slots_b]
        + [pl.BlockSpec((CHUNK, 2 * HD), lambda n: (n, kv_block)), whole((rows, HD)), whole((rows, HD))],
        out_specs=[pl.BlockSpec((rows, CHUNK), lambda n: (0, n)), whole((rows, 2 * HD)), whole((rows, HD))],
        out_shape=[
            shape((rows, width), jnp.bfloat16),
            shape((rows, 2 * HD), jnp.bfloat16),
            shape((rows, HD), jnp.float32),
        ],
        scratch_shapes=[
            pltpu.VMEM((rows, slot_count), jnp.bfloat16),
            pltpu.VMEM((rows, slot_count), jnp.bfloat16),
            pltpu.VMEM((rows, AUX), jnp.float32),
            pltpu.VMEM((rows, AUX), jnp.float32),
            pltpu.VMEM((rows, 2 * HD), jnp.float32),
        ],
        compiler_params=pltpu.CompilerParams(vmem_limit_bytes=VMEM_BYTES),
        name="place",
    )(text_rows, *slots_a, *slots_b, weights, cosine, sine)


GROUP = 2
SOFT = HD ** (-0.5) * LOG2E


def query_kernel(x_ref, weight_ref, scale_ref, cos_ref, sin_ref, kv_ref, start_ref, q_ref, top_ref, sum_ref, acc_ref):
    rows = x_ref.shape[0]
    total = jnp.dot(x_ref[...], weight_ref[...], preferred_element_type=jnp.float32)
    for h in range(GROUP):
        part = total[:, h * HD:(h + 1) * HD] * scale_ref[...]
        q_ref[h * rows:(h + 1) * rows, :] = turned(part, cos_ref[...], sin_ref[...]).astype(jnp.bfloat16)
    scores = lax.dot_general(
        kv_ref[:, :HD], q_ref[...], (((1,), (1,)), ((), ())), preferred_element_type=jnp.float32
    )
    key_at = lax.broadcasted_iota(jnp.int32, (rows, rows), 0)
    query_at = lax.broadcasted_iota(jnp.int32, (rows, rows), 1)
    allowed = (key_at <= query_at) & (key_at >= start_ref[0:1, :])
    scores = jnp.where(jnp.concatenate([allowed] * GROUP, axis=1), scores, BIG_NEG)
    top = jnp.max(scores, axis=0, keepdims=True)
    probs = jnp.exp2((scores - top) * SOFT)
    top_ref[...] = top
    sum_ref[...] = jnp.sum(probs, axis=0, keepdims=True)
    acc_ref[...] = lax.dot_general(
        kv_ref[:, HD:], probs.astype(jnp.bfloat16), (((0,), (0,)), ((), ())), preferred_element_type=jnp.float32
    )


def query(x, weights, scale, cosine, sine, kv, starts, heads):
    rows, width = x.shape
    wide = GROUP * rows
    shape = jax.ShapeDtypeStruct
    return pl.pallas_call(
        query_kernel,
        grid=(heads // GROUP,),
        in_specs=[
            whole((rows, width)),
            pl.BlockSpec((width, GROUP * HD), lambda n: (0, n)),
            whole((rows, HD)),
            whole((rows, HD)),
            whole((rows, HD)),
            whole((rows, 2 * HD)),
            whole((1, rows)),
        ],
        out_specs=[
            pl.BlockSpec((wide, HD), lambda n: (n, 0)),
            pl.BlockSpec((1, wide), lambda n: (0, n)),
            pl.BlockSpec((1, wide), lambda n: (0, n)),
            pl.BlockSpec((HD, wide), lambda n: (0, n)),
        ],
        out_shape=[
            shape((heads * rows, HD), jnp.bfloat16),
            shape((1, heads * rows), jnp.float32),
            shape((1, heads * rows), jnp.float32),
            shape((HD, heads * rows), jnp.float32),
        ],
        compiler_params=pltpu.CompilerParams(vmem_limit_bytes=VMEM_BYTES),
        name="query",
    )(x, weights, scale, cosine, sine, kv, starts)


def attention_kernel(info_ref, q_ref, top_in, sum_in, acc_in, kv_ref, start_ref, out_ref, top_ref, sum_ref, acc_ref):
    rows = out_ref.shape[0]
    heads = out_ref.shape[1] // HD
    groups = heads // GROUP
    wide = GROUP * rows
    me = info_ref[0]
    first = info_ref[1]
    edge = info_ref[2]
    top_ref[...] = top_in[...]
    sum_ref[...] = sum_in[...]
    acc_ref[...] = acc_in[...]

    def block(index, masked):
        keys = kv_ref[index, :, :HD]
        values = kv_ref[index, :, HD:]
        if masked:
            key_at = (index - me) * rows + lax.broadcasted_iota(jnp.int32, (rows, rows), 0)
            allowed = key_at >= start_ref[0:1, :]
            allowed = jnp.concatenate([allowed] * GROUP, axis=1)
        for g in range(groups):
            part = slice(g * wide, (g + 1) * wide)
            scores = lax.dot_general(
                keys, q_ref[part, :], (((1,), (1,)), ((), ())), preferred_element_type=jnp.float32
            )
            if masked:
                scores = jnp.where(allowed, scores, BIG_NEG)
            old = top_ref[:, part]
            top = jnp.maximum(old, jnp.max(scores, axis=0, keepdims=True))
            probs = jnp.exp2((scores - top) * SOFT)
            mixed = lax.dot_general(
                values, probs.astype(jnp.bfloat16), (((0,), (0,)), ((), ())), preferred_element_type=jnp.float32
            )
            shrink = jnp.exp2((old - top) * SOFT)
            top_ref[:, part] = top
            sum_ref[:, part] = sum_ref[:, part] * shrink + jnp.sum(probs, axis=0, keepdims=True)
            acc_ref[:, part] = acc_ref[:, part] * shrink + mixed

    def step(i, _):
        index = me - 1 - i
        needs = index * rows < edge

        @pl.when(needs)
        def _():
            block(index, True)

        @pl.when(jnp.logical_not(needs))
        def _():
            block(index, False)

        return 0

    lax.fori_loop(0, me - first, step, 0)
    for h in range(heads):
        part = slice(h * rows, (h + 1) * rows)
        out_ref[:, h * HD:(h + 1) * HD] = (acc_ref[:, part] / sum_ref[:, part]).T.astype(jnp.bfloat16)


def attend(info, state, kv_all, starts):
    rows = kv_all.shape[1]
    wide = state[0].shape[0]
    vmem = pl.BlockSpec(memory_space=pltpu.VMEM)
    return pl.pallas_call(
        attention_kernel,
        in_specs=[pl.BlockSpec(memory_space=pltpu.SMEM)] + [vmem] * 6,
        out_specs=vmem,
        out_shape=jax.ShapeDtypeStruct((rows, wide // rows * HD), jnp.bfloat16),
        scratch_shapes=[
            pltpu.VMEM((1, wide), jnp.float32),
            pltpu.VMEM((1, wide), jnp.float32),
            pltpu.VMEM((HD, wide), jnp.float32),
        ],
        compiler_params=pltpu.CompilerParams(vmem_limit_bytes=VMEM_BYTES),
        name="attend",
    )(info, *state, kv_all, starts)


def per_device(
    patches,
    merge_up,
    merge_down,
    image_pos,
    text_rows,
    segment,
    query_weight,
    key_weight,
    value_weight,
):
    seq_count = lax.axis_size("seq")
    seq_index = lax.axis_index("seq")
    rows, width = text_rows.shape
    bf16, f32 = jnp.bfloat16, jnp.float32

    with jax.named_scope("weights"):
        weights = lax.all_gather(
            jnp.concatenate([query_weight, key_weight, value_weight], axis=1), "seq", axis=0, tiled=True
        )
        up_other = seq_shift(merge_up, 0, 0, 1)
        down_other = seq_shift(merge_down, 0, 0, 1)

    with jax.named_scope("merger"):
        merged = prepare(patches, segment)
        own = merged.shape[0]
        pair = jnp.concatenate([merged, seq_shift(merged, 0, 1, 0)], axis=0)
        pieces = [pair] + [seq_shift(pair, dx, 0, 0) for dx in range(1, X)]
        outs = merger(pieces, (merge_up, up_other), (merge_down, down_other))
        part_a, part_b = outs[:X], outs[X:]

    with jax.named_scope("sums"):
        got_a = [seq_shift(part_a[dx], -dx, 0, 0) for dx in range(1, X)]
        got_b = seq_shift(part_b[1], 0, 1, 0)
        sum_a = part_a[0] + sum(piece.astype(f32) for piece in got_a)
        sum_b = part_b[0] + got_b.astype(f32)
        last_a = seq_shift(sum_a[own:].astype(bf16), 0, 1, 0)
        last_b = [seq_shift(sum_b[dx * own:(dx + 1) * own].astype(bf16), -dx, 0, 0) for dx in range(1, X)]
        image_a = (sum_a[:own] + last_a.astype(f32)).astype(bf16)
        image_b = (sum_b[:own] + sum(piece.astype(f32) for piece in last_b)).astype(bf16)

    with jax.named_scope("route"):
        target = image_pos // rows
        offset = image_pos % rows
        matches = (target[:, None] == jnp.arange(seq_count, dtype=jnp.int32)[None, :]).astype(jnp.int32)
        slot_rank = jnp.sum((jnp.cumsum(matches, axis=0) - matches) * matches, axis=1)
        slot_index = target * CAP + slot_rank
        select = (slot_index[None, :] == jnp.arange(seq_count * CAP, dtype=jnp.int32)[:, None]).astype(bf16)
        marks = jnp.stack([offset // 128, offset % 128, jnp.ones_like(offset)], axis=1).astype(bf16)
        marks = jnp.pad(marks, ((0, 0), (0, AUX - 3)))
        send = jnp.dot(
            select, jnp.concatenate([image_a, image_b, marks], axis=1), preferred_element_type=f32
        ).astype(bf16)
        got = lax.all_to_all(
            send.reshape(seq_count, CAP, width + AUX), "seq", split_axis=0, concat_axis=0, tiled=True
        ).reshape(seq_count * CAP, width + AUX)
        got_a, got_b = got[:, :HALF_D], got[:, HALF_D:]
        pair_a = jnp.concatenate([got_a, pool_shift(got_a, 0, 1)], axis=0)
        column_b = jnp.concatenate([got_b] + [pool_shift(got_b, dz, 0) for dz in range(1, Z)], axis=0)
        slots_a = [pair_a] + [pool_shift(pair_a, dz, 0) for dz in range(1, Z)]
        slots_b = [column_b, pool_shift(column_b, 0, 1)]

    with jax.named_scope("segments"):
        counted = sum(
            piece[at:at + 1, merge_up.shape[0]:].astype(f32) for piece in pieces for at in range(0, Y * own, own)
        )
        counted = (counted + seq_shift(counted, 0, 0, 1))[0]
        ends = (counted[:3] * 128.0 + counted[3:6]).astype(jnp.int32)
        before = jnp.concatenate([jnp.zeros((1,), jnp.int32), ends])
        starts = jnp.sum(
            jnp.where(segment[None, :] == jnp.arange(4, dtype=jnp.int32)[:, None], before[:, None], 0), axis=0
        )
        info = jnp.stack([seq_index, starts[0] // rows, starts[-1]]).astype(jnp.int32)
        starts = (starts - seq_index * rows)[None, :]

    with jax.named_scope("project"):
        positions = (seq_index * rows + jnp.arange(rows, dtype=jnp.int32)).astype(f32)
        frequency = ROPE_BASE ** (-(jnp.arange(HD // 2, dtype=f32) * 2.0 / HD))
        angles = positions[:, None] * frequency[None, :]
        cosine, sine = jnp.cos(angles), jnp.sin(angles)
        cosine = jnp.concatenate([cosine, cosine], axis=1)
        sine = jnp.concatenate([-sine, sine], axis=1)
        x, kv, scale = place(text_rows, slots_a, slots_b, weights, cosine, sine)
        kv_all = lax.all_gather(kv, "seq", axis=0, tiled=True)
        state = query(x, weights, scale, cosine, sine, kv, starts, query_weight.shape[1] // HD)

    with jax.named_scope("attend"):
        return attend(info, state, kv_all.reshape(seq_count, rows, 2 * HD), starts)


def solution(mesh):
    return jax.shard_map(
        per_device,
        mesh=mesh,
        in_specs=(
            P(("pool", "seq"), None),
            P(None, "seq"),
            P("seq", None),
            P(("pool", "seq")),
            P("seq", None),
            P("seq"),
            P("seq", "pool"),
            P("seq", "pool"),
            P("seq", "pool"),
        ),
        out_specs=P("seq", "pool"),
        check_vma=False,
    )
```

```python
import jax
import jax.numpy as jnp
from jax import lax
from jax.experimental import pallas as pl
from jax.experimental.pallas import tpu as pltpu
from jax.sharding import PartitionSpec as P

HD = 128
CAP = 2
AUX = 128
NORM_EPS = 1e-06
ROPE_BASE = 1000000.0
BIG_NEG = -1e30
LOG2E = 1.4426950408889634
VMEM_BYTES = 56 * 1024 * 1024
X, Y, C = 4, 2, 2
Z, YH = 4, 2
CHUNK = 1024


def rms_rows(matrix):
    return matrix * lax.rsqrt(jnp.mean(matrix * matrix, axis=-1, keepdims=True) + NORM_EPS)


def seq_shift(array, dx, dy, dc):
    pairs = []
    for source in range(X * Y * C):
        x, y, c = source // (Y * C), source // C % Y, source % C
        pairs.append((source, ((x + dx) % X) * Y * C + (y ^ dy) * C + (c ^ dc)))
    return lax.ppermute(array, "seq", pairs)


HALF_D = 4096


def pool_shift(array, dz, dy):
    pairs = []
    for source in range(Z * YH):
        z, y = source // YH, source % YH
        pairs.append((source, ((z + dz) % Z) * YH + (y ^ dy)))
    return lax.ppermute(array, "pool", pairs)


def whole(shape):
    return pl.BlockSpec(shape, lambda n: (0, 0), pipeline_mode=pl.Buffered(1))


def patch_kernel(patches_ref, segment_ref, out_ref):
    own = out_ref.shape[0]
    patch_count, width = patches_ref.shape
    normed = rms_rows(patches_ref[...].astype(jnp.float32)).astype(jnp.bfloat16)
    token = lax.broadcasted_iota(jnp.int32, (own, patch_count), 0)
    patch = lax.broadcasted_iota(jnp.int32, (own, patch_count), 1)
    for k in range(4):
        pick = jnp.where(patch == 4 * token + k, 1.0, 0.0).astype(jnp.bfloat16)
        out_ref[:, k * width:(k + 1) * width] = jnp.dot(
            pick, normed, preferred_element_type=jnp.float32
        ).astype(jnp.bfloat16)
    lane = lax.broadcasted_iota(jnp.int32, (own, AUX), 1)
    marks = jnp.zeros((own, AUX), jnp.float32)
    for v in range(1, 4):
        before = jnp.sum(jnp.where(segment_ref[...] < v, 1.0, 0.0), axis=1, keepdims=True)
        high = jnp.floor(before * (1.0 / 128.0))
        marks += jnp.where(lane == v - 1, high, 0.0) + jnp.where(lane == v + 2, before - 128.0 * high, 0.0)
    out_ref[:, 4 * width:] = marks.astype(jnp.bfloat16)


def prepare(patches, segment):
    vmem = pl.BlockSpec(memory_space=pltpu.VMEM)
    return pl.pallas_call(
        patch_kernel,
        in_specs=[vmem, vmem],
        out_specs=vmem,
        out_shape=jax.ShapeDtypeStruct((patches.shape[0] // 4, 4 * patches.shape[1] + AUX), jnp.bfloat16),
        name="prepare",
    )(patches, segment[None, :])


def merger_kernel(*refs):
    pieces, (up_a, up_b, down_a, down_b), outs = refs[:X], refs[X:X + 4], refs[X + 4:X + 4 + X + Y]
    hidden_ref = refs[-1]
    rows = pieces[0].shape[0]
    depth = up_a.shape[1]
    step = pl.program_id(0)
    half = pl.num_programs(0) // 2

    @pl.when(step == 0)
    def _():
        merged = jnp.concatenate([piece[:, :depth] for piece in pieces], axis=0)
        up = jnp.concatenate([up_a[...], up_b[...]], axis=0)
        value = lax.dot_general(merged, up, (((1,), (1,)), ((), ())), preferred_element_type=jnp.float32)
        value = 0.5 * value * (1.0 + lax.erf(value * (0.5 ** 0.5)))
        hidden_ref[...] = value.astype(jnp.bfloat16)

    down = jnp.concatenate([down_a[...], down_b[...]], axis=0)
    total = jnp.dot(hidden_ref[...], down, preferred_element_type=jnp.float32)

    @pl.when(step < half)
    def _():
        for dx in range(X):
            outs[dx][...] = total[dx * rows:(dx + 1) * rows].astype(outs[dx].dtype)

    @pl.when(step >= half)
    def _():
        own = rows // Y
        for dx in range(X):
            for dy in range(Y):
                at = dx * rows + dy * own
                outs[X + dy][dx * own:(dx + 1) * own, :] = total[at:at + own].astype(outs[X + dy].dtype)


def merger(pieces, ups, downs):
    rows = pieces[0].shape[0]
    units, depth = ups[0].shape
    width = downs[0].shape[1]
    block = 1024
    half = HALF_D // block
    first = lambda shape: pl.BlockSpec(shape, lambda n: (0, jnp.minimum(n, half - 1)))
    second = lambda shape: pl.BlockSpec(shape, lambda n: (0, jnp.maximum(n - half, 0)))
    own = rows // Y
    shape = jax.ShapeDtypeStruct
    return pl.pallas_call(
        merger_kernel,
        grid=(width // block,),
        in_specs=[whole(pieces[0].shape)] * X
        + [whole((units, depth))] * 2
        + [pl.BlockSpec((units, block), lambda n: (0, n))] * 2,
        out_specs=[first((rows, block))] * X + [second((X * own, block))] * Y,
        out_shape=[shape((rows, HALF_D), jnp.float32 if dx == 0 else jnp.bfloat16) for dx in range(X)]
        + [shape((X * own, width - HALF_D), jnp.float32 if dy == 0 else jnp.bfloat16) for dy in range(Y)],
        scratch_shapes=[pltpu.VMEM((X * rows, 2 * units), jnp.bfloat16)],
        compiler_params=pltpu.CompilerParams(vmem_limit_bytes=VMEM_BYTES),
        name="merger",
    )(*pieces, *ups, *downs)


def turned(part, cosine, sine):
    return part * cosine + pltpu.roll(part, HD // 2, 1) * sine


def slot_marks(b0, b1):
    cap = b0.shape[0] // Z
    at = b0.shape[1] - AUX
    blocks = []
    for dz in range(Z):
        for ref in (b0, b1):
            blocks.append(ref[dz * cap:(dz + 1) * cap, at:])
    return jnp.concatenate(blocks, axis=0), jnp.concatenate([b0[:, at:], b1[:, at:]], axis=0)


def slot_pick(marks, rows):
    value = marks.astype(jnp.float32)
    offset = value[:, 0:1] * 128.0 + value[:, 1:2]
    offset = jnp.where(value[:, 2:3] > 0.5, offset, -1.0).astype(jnp.int32)
    token = lax.broadcasted_iota(jnp.int32, (value.shape[0], rows), 1)
    return jnp.where(offset == token, 1.0, 0.0).T.astype(jnp.bfloat16)


def lane_sums(matrix):
    total = matrix[:, :HD]
    for at in range(HD, matrix.shape[1], HD):
        total += matrix[:, at:at + HD]
    return total


def text_kernel(text_ref, weight_ref, kv_ref, total_ref):
    @pl.when(pl.program_id(0) == 0)
    def _():
        kv_ref[...] = jnp.zeros_like(kv_ref)
        total_ref[...] = jnp.zeros_like(total_ref)

    kv_ref[...] += jnp.dot(text_ref[...], weight_ref[...], preferred_element_type=jnp.float32)
    value = text_ref[...].astype(jnp.float32)
    total_ref[...] += lane_sums(value * value)


def project_text(text_rows, weights):
    rows, width = text_rows.shape
    kv_block = weights.shape[1] // (2 * HD) - 1
    shape = jax.ShapeDtypeStruct
    return pl.pallas_call(
        text_kernel,
        grid=(width // CHUNK,),
        in_specs=[
            pl.BlockSpec((rows, CHUNK), lambda n: (0, n)),
            pl.BlockSpec((CHUNK, 2 * HD), lambda n: (n, kv_block)),
        ],
        out_specs=[whole((rows, 2 * HD)), whole((rows, HD))],
        out_shape=[shape((rows, 2 * HD), jnp.float32), shape((rows, HD), jnp.float32)],
        compiler_params=pltpu.CompilerParams(vmem_limit_bytes=VMEM_BYTES),
        name="project_text",
    )(text_rows, weights)


def slot_kernel(
    a0, a1, a2, a3, b0, b1, weight_ref, text_kv_ref, text_total_ref, cos_ref, sin_ref,
    kv_ref, scale_ref, sum_ref, total_ref,
):
    rows = text_kv_ref.shape[0]
    step = pl.program_id(0)
    steps = pl.num_programs(0)
    half = HALF_D // CHUNK
    width = steps * CHUNK

    @pl.when(step == 0)
    def _():
        sum_ref[...] = jnp.zeros_like(sum_ref)
        total_ref[...] = jnp.zeros_like(total_ref)

    def add(at, refs, index):
        part = pl.ds(pl.multiple_of(index * CHUNK, CHUNK), CHUNK)
        slots = jnp.concatenate([ref[:, part] for ref in refs], axis=0)
        sum_ref[at] += jnp.dot(slots, weight_ref[...], preferred_element_type=jnp.float32)
        value = slots.astype(jnp.float32)
        total_ref[at] += lane_sums(value * value)

    @pl.when(step < half)
    def _():
        add(0, (a0, a1, a2, a3), step)

    @pl.when(step >= half)
    def _():
        add(1, (b0, b1), step - half)

    @pl.when(step == steps - 1)
    def _():
        marks = slot_marks(b0, b1)[1]
        pick = slot_pick(marks, rows)
        held = jnp.dot(pick, marks, preferred_element_type=jnp.float32)[:, 2:3] > 0.5
        cap = marks.shape[0] // (Z * YH)

        def joined(ref):
            first = [
                ref[0, (dz * YH + yh) * cap:(dz * YH + yh + 1) * cap, :] for yh in range(YH) for dz in range(Z)
            ]
            return jnp.concatenate(first, axis=0) + ref[1]

        def placed(value):
            high = value.astype(jnp.bfloat16)
            low = (value - high.astype(jnp.float32)).astype(jnp.bfloat16)
            return jnp.dot(pick, high, preferred_element_type=jnp.float32) + jnp.dot(
                pick, low, preferred_element_type=jnp.float32
            )

        def scale_of(total):
            return lax.rsqrt(jnp.sum(total, axis=1, keepdims=True) / width + NORM_EPS)

        slot_scale = scale_of(joined(total_ref))
        text_scale = scale_of(text_total_ref[...])
        slot_scale = jnp.broadcast_to(slot_scale, (slot_scale.shape[0], HD))
        scale = jnp.where(held, placed(slot_scale), text_scale)
        scale_ref[...] = scale
        kv = jnp.where(held, placed(joined(sum_ref)), text_kv_ref[...])
        kv_ref[:, :HD] = turned(kv[:, :HD] * scale, cos_ref[...], sin_ref[...]).astype(jnp.bfloat16)
        kv_ref[:, HD:] = (kv[:, HD:] * scale).astype(jnp.bfloat16)


def project_slots(slots_a, slots_b, weights, text_kv, text_total, cosine, sine):
    rows = text_kv.shape[0]
    width = weights.shape[0]
    slot_count = X * slots_a[0].shape[0]
    kv_block = weights.shape[1] // (2 * HD) - 1
    shape = jax.ShapeDtypeStruct
    return pl.pallas_call(
        slot_kernel,
        grid=(width // CHUNK,),
        in_specs=[whole(piece.shape) for piece in slots_a]
        + [whole(piece.shape) for piece in slots_b]
        + [pl.BlockSpec((CHUNK, 2 * HD), lambda n: (n, kv_block))]
        + [whole((rows, 2 * HD)), whole((rows, HD)), whole((rows, HD)), whole((rows, HD))],
        out_specs=[whole((rows, 2 * HD)), whole((rows, HD))],
        out_shape=[shape((rows, 2 * HD), jnp.bfloat16), shape((rows, HD), jnp.float32)],
        scratch_shapes=[
            pltpu.VMEM((2, slot_count, 2 * HD), jnp.float32),
            pltpu.VMEM((2, slot_count, HD), jnp.float32),
        ],
        compiler_params=pltpu.CompilerParams(vmem_limit_bytes=VMEM_BYTES),
        name="project_slots",
    )(*slots_a, *slots_b, weights, text_kv, text_total, cosine, sine)


GROUP = 2
SOFT = HD ** (-0.5) * LOG2E
LIMIT = 60.0


def query_kernel(
    text_ref, a0, a1, a2, a3, b0, b1, weight_ref, scale_ref, cos_ref, sin_ref, kv_ref, start_ref,
    q_ref, top_ref, sum_ref, acc_ref, pick_a, pick_b, held_ref, total_ref,
):
    rows = text_ref.shape[0]
    step = pl.program_id(0)
    steps = pl.num_programs(0)
    half = HALF_D // CHUNK
    wide = GROUP * rows

    @pl.when(step == 0)
    def _():
        marks_a, marks_b = slot_marks(b0, b1)
        pick_a[...] = slot_pick(marks_a, rows)
        pick_b[...] = slot_pick(marks_b, rows)
        held_ref[...] = jnp.dot(pick_b[...], marks_b, preferred_element_type=jnp.float32)
        total_ref[...] = jnp.zeros_like(total_ref)

    def add(pick, refs, index):
        part = pl.ds(pl.multiple_of(index * CHUNK, CHUNK), CHUNK)
        slots = jnp.concatenate([ref[:, part] for ref in refs], axis=0)
        image = jnp.dot(pick[...], slots, preferred_element_type=jnp.float32)
        mixed = jnp.where(held_ref[:, 2:3] > 0.5, image, text_ref[...].astype(jnp.float32)).astype(jnp.bfloat16)
        total_ref[...] += jnp.dot(mixed, weight_ref[...], preferred_element_type=jnp.float32)

    @pl.when(step < half)
    def _():
        add(pick_a, (a0, a1, a2, a3), step)

    @pl.when(step >= half)
    def _():
        add(pick_b, (b0, b1), step - half)

    @pl.when(step == steps - 1)
    def _():
        heads = total_ref.shape[1] // HD
        for h in range(heads):
            part = total_ref[:, h * HD:(h + 1) * HD] * scale_ref[...]
            q_ref[h * rows:(h + 1) * rows, :] = turned(part, cos_ref[...], sin_ref[...]).astype(jnp.bfloat16)
        key_at = lax.broadcasted_iota(jnp.int32, (rows, rows), 0)
        query_at = lax.broadcasted_iota(jnp.int32, (rows, rows), 1)
        allowed = (key_at <= query_at) & (key_at >= start_ref[0:1, :])
        allowed = jnp.concatenate([allowed] * GROUP, axis=1)
        for g in range(heads // GROUP):
            part = slice(g * wide, (g + 1) * wide)
            scores = lax.dot_general(
                kv_ref[:, :HD], q_ref[part, :], (((1,), (1,)), ((), ())), preferred_element_type=jnp.float32
            )
            scores = jnp.where(allowed, scores, BIG_NEG)
            top = jnp.max(scores, axis=0, keepdims=True)
            probs = jnp.exp2((scores - top) * SOFT)
            top_ref[:, part] = top
            sum_ref[:, part] = jnp.sum(probs, axis=0, keepdims=True)
            acc_ref[:, part] = lax.dot_general(
                kv_ref[:, HD:], probs.astype(jnp.bfloat16), (((0,), (0,)), ((), ())),
                preferred_element_type=jnp.float32,
            )


def query(text_rows, slots_a, slots_b, weights, scale, cosine, sine, kv, starts, heads):
    rows, width = text_rows.shape
    slot_count = X * slots_a[0].shape[0]
    wide = heads * rows
    shape = jax.ShapeDtypeStruct
    return pl.pallas_call(
        query_kernel,
        grid=(width // CHUNK,),
        in_specs=[pl.BlockSpec((rows, CHUNK), lambda n: (0, n))]
        + [whole(piece.shape) for piece in slots_a]
        + [whole(piece.shape) for piece in slots_b]
        + [pl.BlockSpec((CHUNK, heads * HD), lambda n: (n, 0))]
        + [whole((rows, HD))] * 3
        + [whole((rows, 2 * HD)), whole((1, rows))],
        out_specs=[whole((wide, HD)), whole((1, wide)), whole((1, wide)), whole((HD, wide))],
        out_shape=[
            shape((wide, HD), jnp.bfloat16),
            shape((1, wide), jnp.float32),
            shape((1, wide), jnp.float32),
            shape((HD, wide), jnp.float32),
        ],
        scratch_shapes=[
            pltpu.VMEM((rows, slot_count), jnp.bfloat16),
            pltpu.VMEM((rows, slot_count), jnp.bfloat16),
            pltpu.VMEM((rows, AUX), jnp.float32),
            pltpu.VMEM((rows, heads * HD), jnp.float32),
        ],
        compiler_params=pltpu.CompilerParams(vmem_limit_bytes=VMEM_BYTES),
        name="query",
    )(text_rows, *slots_a, *slots_b, weights, scale, cosine, sine, kv, starts)


def attention_kernel(
    info_ref, q_ref, top_in, sum_in, acc_in, kv_ref, start_ref, out_ref, base_ref, top_ref, sum_ref, acc_ref
):
    rows = out_ref.shape[0]
    heads = out_ref.shape[1] // HD
    wide = GROUP * rows
    me = info_ref[0]
    first = info_ref[1]
    edge = info_ref[2]
    count = me - first

    def allowed_keys(indices):
        masks = []
        for index in indices:
            key_at = (index - me) * rows + lax.broadcasted_iota(jnp.int32, (rows, rows), 0)
            masks.append(key_at >= start_ref[0:1, :])
        return jnp.concatenate([jnp.concatenate(masks, axis=0)] * GROUP, axis=1)

    def loaded(indices):
        keys = jnp.concatenate([kv_ref[index, :, :HD] for index in indices], axis=0)
        values = jnp.concatenate([kv_ref[index, :, HD:] for index in indices], axis=0)
        return keys, values

    def scores_of(keys, part, allowed):
        scores = lax.dot_general(
            keys, q_ref[part, :], (((1,), (1,)), ((), ())), preferred_element_type=jnp.float32
        )
        return scores if allowed is None else jnp.where(allowed, scores, BIG_NEG)

    def mixed_of(values, probs):
        return lax.dot_general(
            values, probs.astype(jnp.bfloat16), (((0,), (0,)), ((), ())), preferred_element_type=jnp.float32
        )

    def fast(indices, masked):
        keys, values = loaded(indices)
        allowed = allowed_keys(indices) if masked else None
        for g in range(heads // GROUP):
            part = slice(g * wide, (g + 1) * wide)
            scores = scores_of(keys, part, allowed)
            top_ref[:, part] = jnp.maximum(top_ref[:, part], jnp.max(scores, axis=0, keepdims=True))
            probs = jnp.exp2(scores * SOFT - base_ref[:, part])
            acc_ref[:, part] += mixed_of(values, probs)
            sum_ref[:, part] += jnp.sum(probs, axis=0, keepdims=True)

    def slow(index):
        keys, values = loaded([index])
        allowed = allowed_keys([index])
        for g in range(heads // GROUP):
            part = slice(g * wide, (g + 1) * wide)
            scores = scores_of(keys, part, allowed)
            old = top_ref[:, part]
            top = jnp.maximum(old, jnp.max(scores, axis=0, keepdims=True))
            probs = jnp.exp2((scores - top) * SOFT)
            shrink = jnp.exp2((old - top) * SOFT)
            top_ref[:, part] = top
            sum_ref[:, part] = sum_ref[:, part] * shrink + jnp.sum(probs, axis=0, keepdims=True)
            acc_ref[:, part] = acc_ref[:, part] * shrink + mixed_of(values, probs)

    def start():
        top_ref[...] = top_in[...]
        sum_ref[...] = sum_in[...]
        acc_ref[...] = acc_in[...]

    def either(indices):
        needs = indices[-1] * rows < edge

        @pl.when(needs)
        def _():
            fast(indices, True)

        @pl.when(jnp.logical_not(needs))
        def _():
            fast(indices, False)

    start()
    base_ref[...] = top_in[...] * SOFT
    odd = count % 2

    @pl.when(odd == 1)
    def _():
        either([me - 1])

    def pair(i, _):
        at = me - 1 - odd - 2 * i
        either([at, at - 1])
        return 0

    lax.fori_loop(0, count // 2, pair, 0)
    grown = jnp.max(top_ref[...] * SOFT - base_ref[...])

    @pl.when(grown > LIMIT)
    def _():
        start()

        def again(i, _):
            slow(me - 1 - i)
            return 0

        lax.fori_loop(0, count, again, 0)

    for h in range(heads):
        part = slice(h * rows, (h + 1) * rows)
        out_ref[:, h * HD:(h + 1) * HD] = (acc_ref[:, part] / sum_ref[:, part]).T.astype(jnp.bfloat16)


def attend(info, state, kv_all, starts):
    rows = kv_all.shape[1]
    wide = state[0].shape[0]
    vmem = pl.BlockSpec(memory_space=pltpu.VMEM)
    return pl.pallas_call(
        attention_kernel,
        in_specs=[pl.BlockSpec(memory_space=pltpu.SMEM)] + [vmem] * 6,
        out_specs=vmem,
        out_shape=jax.ShapeDtypeStruct((rows, wide // rows * HD), jnp.bfloat16),
        scratch_shapes=[
            pltpu.VMEM((1, wide), jnp.float32),
            pltpu.VMEM((1, wide), jnp.float32),
            pltpu.VMEM((1, wide), jnp.float32),
            pltpu.VMEM((HD, wide), jnp.float32),
        ],
        compiler_params=pltpu.CompilerParams(vmem_limit_bytes=VMEM_BYTES),
        name="attend",
    )(info, *state, kv_all, starts)


def per_device(
    patches,
    merge_up,
    merge_down,
    image_pos,
    text_rows,
    segment,
    query_weight,
    key_weight,
    value_weight,
):
    seq_count = lax.axis_size("seq")
    seq_index = lax.axis_index("seq")
    rows, width = text_rows.shape
    bf16, f32 = jnp.bfloat16, jnp.float32

    with jax.named_scope("merger"):
        up_other = seq_shift(merge_up.T, 0, 0, 1)
        down_other = seq_shift(merge_down, 0, 0, 1)
        merged = prepare(patches, segment)
        own = merged.shape[0]
        beside = seq_shift(merged, 0, 1, 0)
        merged, query_weight, key_weight, value_weight = lax.optimization_barrier(
            (merged, query_weight, key_weight, value_weight)
        )
        weights = lax.all_gather(
            jnp.concatenate([query_weight, key_weight, value_weight], axis=1), "seq", axis=0, tiled=True
        )
        pair = jnp.concatenate([merged, beside], axis=0)
        pieces = [pair] + [seq_shift(pair, dx, 0, 0) for dx in range(1, X)]
        outs = merger(pieces, (merge_up.T, up_other), (merge_down, down_other))
        part_a, part_b = outs[:X], outs[X:]

    with jax.named_scope("sums"):
        got_a = [seq_shift(part_a[dx], -dx, 0, 0) for dx in range(1, X)]
        got_b = seq_shift(part_b[1], 0, 1, 0)
        sum_a = part_a[0] + sum(piece.astype(f32) for piece in got_a)
        sum_b = part_b[0] + got_b.astype(f32)
        last_a = seq_shift(sum_a[own:].astype(bf16), 0, 1, 0)
        last_b = [seq_shift(sum_b[dx * own:(dx + 1) * own].astype(bf16), -dx, 0, 0) for dx in range(1, X)]
        image_a = (sum_a[:own] + last_a.astype(f32)).astype(bf16)
        image_b = (sum_b[:own] + sum(piece.astype(f32) for piece in last_b)).astype(bf16)

    with jax.named_scope("segments"):
        counted = sum(
            piece[at:at + 1, merge_up.shape[0]:].astype(f32) for piece in pieces for at in range(0, Y * own, own)
        )
        counted = (counted + seq_shift(counted, 0, 0, 1))[0]
        ends = (counted[:3] * 128.0 + counted[3:6]).astype(jnp.int32)
        before = jnp.concatenate([jnp.zeros((1,), jnp.int32), ends])
        starts = jnp.sum(
            jnp.where(segment[None, :] == jnp.arange(4, dtype=jnp.int32)[:, None], before[:, None], 0), axis=0
        )
        info = jnp.stack([seq_index, starts[0] // rows, starts[-1]]).astype(jnp.int32)
        starts = (starts - seq_index * rows)[None, :]

    with jax.named_scope("angles"):
        positions = (seq_index * rows + jnp.arange(rows, dtype=jnp.int32)).astype(f32)
        frequency = ROPE_BASE ** (-(jnp.arange(HD // 2, dtype=f32) * 2.0 / HD))
        angles = positions[:, None] * frequency[None, :]
        cosine, sine = jnp.cos(angles), jnp.sin(angles)
        cosine = jnp.concatenate([cosine, cosine], axis=1)
        sine = jnp.concatenate([-sine, sine], axis=1)

    with jax.named_scope("route"):
        target = image_pos // rows
        offset = image_pos % rows
        matches = (target[:, None] == jnp.arange(seq_count, dtype=jnp.int32)[None, :]).astype(jnp.int32)
        slot_rank = jnp.sum((jnp.cumsum(matches, axis=0) - matches) * matches, axis=1)
        slot_index = target * CAP + slot_rank
        select = (slot_index[None, :] == jnp.arange(seq_count * CAP, dtype=jnp.int32)[:, None]).astype(bf16)
        marks = jnp.stack([offset // 128, offset % 128, jnp.ones_like(offset)], axis=1).astype(bf16)
        marks = jnp.pad(marks, ((0, 0), (0, AUX - 3)))
        send = jnp.dot(
            select, jnp.concatenate([image_a, image_b, marks], axis=1), preferred_element_type=f32
        ).astype(bf16)
        got = lax.all_to_all(
            send.reshape(seq_count, CAP, width + AUX), "seq", split_axis=0, concat_axis=0, tiled=True
        ).reshape(seq_count * CAP, width + AUX)
        got, info, starts, cosine, sine = lax.optimization_barrier((got, info, starts, cosine, sine))
        got_a, got_b = got[:, :HALF_D], got[:, HALF_D:]
        pair_a = jnp.concatenate([got_a, pool_shift(got_a, 0, 1)], axis=0)
        column_b = jnp.concatenate([got_b] + [pool_shift(got_b, dz, 0) for dz in range(1, Z)], axis=0)
        slots_a = [pair_a] + [pool_shift(pair_a, dz, 0) for dz in range(1, Z)]
        slots_b = [column_b, pool_shift(column_b, 0, 1)]

    with jax.named_scope("project"):
        text_kv, text_total = project_text(text_rows, weights)
        kv, scale = project_slots(slots_a, slots_b, weights, text_kv, text_total, cosine, sine)
        kv_all = lax.all_gather(kv, "seq", axis=0, tiled=True)
        state = query(
            text_rows, slots_a, slots_b, weights, scale, cosine, sine, kv, starts, query_weight.shape[1] // HD
        )

    with jax.named_scope("attend"):
        return attend(info, state, kv_all.reshape(seq_count, rows, 2 * HD), starts)


def solution(mesh):
    return jax.shard_map(
        per_device,
        mesh=mesh,
        in_specs=(
            P(("pool", "seq"), None),
            P(None, "seq"),
            P("seq", None),
            P(("pool", "seq")),
            P("seq", None),
            P("seq"),
            P("seq", "pool"),
            P("seq", "pool"),
            P("seq", "pool"),
        ),
        out_specs=P("seq", "pool"),
        check_vma=False,
    )
```

```python
import jax
import jax.numpy as jnp
from jax import lax
from jax.experimental import pallas as pl
from jax.experimental.pallas import tpu as pltpu
from jax.sharding import PartitionSpec as P

HD = 128
CAP = 2
AUX = 128
NORM_EPS = 1e-06
ROPE_BASE = 1000000.0
BIG_NEG = -1e30
LOG2E = 1.4426950408889634
VMEM_BYTES = 56 * 1024 * 1024
X, Y, C = 4, 2, 2
Z, YH = 4, 2
CHUNK = 1024


def rms_rows(matrix):
    return matrix * lax.rsqrt(jnp.mean(matrix * matrix, axis=-1, keepdims=True) + NORM_EPS)


def seq_shift(array, dx, dy, dc):
    pairs = []
    for source in range(X * Y * C):
        x, y, c = source // (Y * C), source // C % Y, source % C
        pairs.append((source, ((x + dx) % X) * Y * C + (y ^ dy) * C + (c ^ dc)))
    return lax.ppermute(array, "seq", pairs)


HALF_D = 4096


def pool_shift(array, dz, dy):
    pairs = []
    for source in range(Z * YH):
        z, y = source // YH, source % YH
        pairs.append((source, ((z + dz) % Z) * YH + (y ^ dy)))
    return lax.ppermute(array, "pool", pairs)


def whole(shape):
    return pl.BlockSpec(shape, lambda n: (0, 0), pipeline_mode=pl.Buffered(1))


def patch_kernel(patches_ref, segment_ref, out_ref):
    own = out_ref.shape[0]
    patch_count, width = patches_ref.shape
    normed = rms_rows(patches_ref[...].astype(jnp.float32)).astype(jnp.bfloat16)
    token = lax.broadcasted_iota(jnp.int32, (own, patch_count), 0)
    patch = lax.broadcasted_iota(jnp.int32, (own, patch_count), 1)
    for k in range(4):
        pick = jnp.where(patch == 4 * token + k, 1.0, 0.0).astype(jnp.bfloat16)
        out_ref[:, k * width:(k + 1) * width] = jnp.dot(
            pick, normed, preferred_element_type=jnp.float32
        ).astype(jnp.bfloat16)
    lane = lax.broadcasted_iota(jnp.int32, (own, AUX), 1)
    marks = jnp.zeros((own, AUX), jnp.float32)
    for v in range(1, 4):
        before = jnp.sum(jnp.where(segment_ref[...] < v, 1.0, 0.0), axis=1, keepdims=True)
        high = jnp.floor(before * (1.0 / 128.0))
        marks += jnp.where(lane == v - 1, high, 0.0) + jnp.where(lane == v + 2, before - 128.0 * high, 0.0)
    out_ref[:, 4 * width:] = marks.astype(jnp.bfloat16)


def prepare(patches, segment):
    vmem = pl.BlockSpec(memory_space=pltpu.VMEM)
    return pl.pallas_call(
        patch_kernel,
        in_specs=[vmem, vmem],
        out_specs=vmem,
        out_shape=jax.ShapeDtypeStruct((patches.shape[0] // 4, 4 * patches.shape[1] + AUX), jnp.bfloat16),
        name="prepare",
    )(patches, segment[None, :])


ANY = pl.BlockSpec(memory_space=pl.ANY)
VMEM = pl.BlockSpec(memory_space=pltpu.VMEM)
SMEM = pl.BlockSpec(memory_space=pltpu.SMEM)


def merger_kernel(*refs):
    (near, far, up_a, up_b, down_a, down_b), outs = refs[:6], refs[6:6 + X + Y]
    up_ref, down_ref, sems = refs[6 + X + Y:]
    units, depth = up_a.shape
    own = near.shape[0] // X
    halves = [slice(0, HALF_D), slice(HALF_D, down_a.shape[1])]
    copies = []
    for at, source in enumerate((up_a, up_b)):
        copies.append(pltpu.make_async_copy(source, up_ref.at[pl.ds(at * units, units), :], sems.at[at]))
    for n, half in enumerate(halves):
        for at, source in enumerate((down_a, down_b)):
            copies.append(
                pltpu.make_async_copy(
                    source.at[:, half], down_ref.at[pl.ds(at * units, units), half], sems.at[2 + 2 * n + at]
                )
            )
    for copy in copies:
        copy.start()
    merged = jnp.concatenate([near[:, :depth], far[:, :depth]], axis=0)
    hidden = []
    for at in range(2):
        copies[at].wait()
        value = lax.dot_general(
            merged, up_ref[at * units:(at + 1) * units, :], (((1,), (1,)), ((), ())),
            preferred_element_type=jnp.float32,
        )
        hidden.append((0.5 * value * (1.0 + lax.erf(value * (0.5 ** 0.5)))).astype(jnp.bfloat16))
    hidden = jnp.concatenate(hidden, axis=1)
    for n, half in enumerate(halves):
        copies[2 + 2 * n].wait()
        copies[3 + 2 * n].wait()
        for start in range(half.start, half.stop, CHUNK):
            total = jnp.dot(hidden, down_ref[:, start:start + CHUNK], preferred_element_type=jnp.float32)
            part = slice(start - half.start, start - half.start + CHUNK)
            if n == 0:
                for dx in range(X):
                    for dy in range(Y):
                        at = dy * X * own + dx * own
                        outs[dx][dy * own:(dy + 1) * own, part] = total[at:at + own].astype(outs[dx].dtype)
            else:
                for dy in range(Y):
                    at = dy * X * own
                    outs[X + dy][:, part] = total[at:at + X * own].astype(outs[X + dy].dtype)


def merger(near, far, ups, downs):
    units, depth = ups[0].shape
    width = downs[0].shape[1]
    own = near.shape[0] // X
    shape = jax.ShapeDtypeStruct
    return pl.pallas_call(
        merger_kernel,
        in_specs=[VMEM, VMEM] + [ANY] * 4,
        out_specs=[VMEM] * (X + Y),
        out_shape=[shape((Y * own, HALF_D), jnp.float32 if dx == 0 else jnp.bfloat16) for dx in range(X)]
        + [shape((X * own, width - HALF_D), jnp.float32 if dy == 0 else jnp.bfloat16) for dy in range(Y)],
        scratch_shapes=[
            pltpu.VMEM((2 * units, depth), jnp.bfloat16),
            pltpu.VMEM((2 * units, width), jnp.bfloat16),
            pltpu.SemaphoreType.DMA((6,)),
        ],
        compiler_params=pltpu.CompilerParams(vmem_limit_bytes=VMEM_BYTES),
        name="merger",
    )(near, far, *ups, *downs)


def turned(part, cosine, sine):
    return part * cosine + pltpu.roll(part, HD // 2, 1) * sine


ARRAYS = 5
SHARDS = []
for _dc in range(C):
    for _array, (_dx, _dys) in enumerate([(0, (0, 1)), (3, (0, 1)), (1, (0, 1)), (2, (0,)), (2, (1,))]):
        for _block, _dy in enumerate(_dys):
            SHARDS.append((_dc * ARRAYS + _array, _block, _dx, _dy, _dc))
SPLIT = 384


def weight_copies(sources, target, sems, columns, at):
    depth = target.shape[1]
    copies = []
    for n, (array, block, _, _, _) in enumerate(SHARDS):
        source = sources[array].at[pl.ds(block * depth, depth), columns]
        wide = columns.stop - columns.start
        copies.append(pltpu.make_async_copy(source, target.at[n, :, pl.ds(at, wide)], sems.at[n]))
    return copies


def slot_copies(pieces, target, sems):
    first, second = pieces[:Z], pieces[Z:]
    cap = first[0].shape[0] // YH
    copies = []
    for dz in range(Z):
        copies.append((first[dz], target.at[pl.ds(dz * YH * cap, YH * cap), pl.ds(0, HALF_D)]))
        for yh in range(YH):
            source = second[yh].at[pl.ds(dz * cap, cap), :]
            copies.append(
                (source, target.at[pl.ds((dz * YH + yh) * cap, cap), pl.ds(HALF_D, second[yh].shape[1])])
            )
    return [pltpu.make_async_copy(source, to, sems.at[n]) for n, (source, to) in enumerate(copies)]


SLOT_COPIES = Z * (1 + YH)


def slot_pick(marks, rows):
    value = marks.astype(jnp.float32)
    offset = value[:, 0:1] * 128.0 + value[:, 1:2]
    offset = jnp.where(value[:, 2:3] > 0.5, offset, -1.0).astype(jnp.int32)
    token = lax.broadcasted_iota(jnp.int32, (value.shape[0], rows), 1)
    return jnp.where(offset == token, 1.0, 0.0).T.astype(jnp.bfloat16)


def lane_sums(matrix):
    total = matrix[:, :HD]
    for at in range(HD, matrix.shape[1], HD):
        total += matrix[:, at:at + HD]
    return total


def columns_of(order_ref, n, depth):
    return pl.ds(pl.multiple_of(order_ref[n] * depth, depth), depth)


def text_kernel(*refs):
    order_ref, text_ref, sources = refs[0], refs[1], refs[2:2 + C * ARRAYS]
    kv_ref, total_ref, weight_ref, sems = refs[2 + C * ARRAYS:]
    copies = weight_copies(sources, weight_ref, sems, slice(0, 2 * HD), 0)
    for copy in copies:
        copy.start()
    depth = weight_ref.shape[1]
    total = jnp.zeros(total_ref.shape, jnp.float32)
    for start in range(0, text_ref.shape[1], CHUNK):
        value = text_ref[:, start:start + CHUNK].astype(jnp.float32)
        total += lane_sums(value * value)
    total_ref[...] = total
    kv = jnp.zeros(kv_ref.shape, jnp.float32)
    for n, copy in enumerate(copies):
        copy.wait()
        kv += jnp.dot(
            text_ref[:, columns_of(order_ref, n, depth)], weight_ref[n], preferred_element_type=jnp.float32
        )
    kv_ref[...] = kv


def project_text(order, text_rows, weights):
    rows, width = text_rows.shape
    shape = jax.ShapeDtypeStruct
    return pl.pallas_call(
        text_kernel,
        in_specs=[SMEM, VMEM] + [ANY] * len(weights),
        out_specs=[VMEM, VMEM],
        out_shape=[shape((rows, 2 * HD), jnp.float32), shape((rows, HD), jnp.float32)],
        scratch_shapes=[
            pltpu.VMEM((len(SHARDS), width // len(SHARDS), 2 * HD), jnp.bfloat16),
            pltpu.SemaphoreType.DMA((len(SHARDS),)),
        ],
        compiler_params=pltpu.CompilerParams(vmem_limit_bytes=VMEM_BYTES),
        name="project_text",
    )(order, text_rows, *weights)


def slot_kernel(*refs):
    order_ref, pieces, refs = refs[0], refs[1:1 + Z + YH], refs[1 + Z + YH:]
    sources, refs = refs[:C * ARRAYS], refs[C * ARRAYS:]
    text_kv_ref, text_total_ref, cos_ref, sin_ref, kv_ref, scale_ref = refs[:6]
    slots_ref, weight_ref, slot_sems, sems = refs[6:]
    rows = text_kv_ref.shape[0]
    width = slots_ref.shape[1] - AUX
    loads = slot_copies(pieces, slots_ref, slot_sems)
    copies = weight_copies(sources, weight_ref, sems, slice(0, 2 * HD), 0)
    for copy in loads + copies:
        copy.start()
    for copy in loads:
        copy.wait()
    marks = slots_ref[:, width:]
    pick = slot_pick(marks, rows)
    held = jnp.dot(pick, marks, preferred_element_type=jnp.float32)[:, 2:3] > 0.5
    depth = weight_ref.shape[1]
    total = jnp.zeros((slots_ref.shape[0], HD), jnp.float32)
    kv = jnp.zeros((slots_ref.shape[0], 2 * HD), jnp.float32)
    for n, copy in enumerate(copies):
        copy.wait()
        slots = slots_ref[:, columns_of(order_ref, n, depth)]
        kv += jnp.dot(slots, weight_ref[n], preferred_element_type=jnp.float32)
        value = slots.astype(jnp.float32)
        total += lane_sums(value * value)

    def placed(value):
        high = value.astype(jnp.bfloat16)
        low = (value - high.astype(jnp.float32)).astype(jnp.bfloat16)
        return jnp.dot(pick, high, preferred_element_type=jnp.float32) + jnp.dot(
            pick, low, preferred_element_type=jnp.float32
        )

    def scale_of(total):
        return lax.rsqrt(jnp.sum(total, axis=1, keepdims=True) / width + NORM_EPS)

    slot_scale = jnp.broadcast_to(scale_of(total), (total.shape[0], HD))
    scale = jnp.where(held, placed(slot_scale), scale_of(text_total_ref[...]))
    scale_ref[...] = scale
    kv = jnp.where(held, placed(kv), text_kv_ref[...])
    kv_ref[:, :HD] = turned(kv[:, :HD] * scale, cos_ref[...], sin_ref[...]).astype(jnp.bfloat16)
    kv_ref[:, HD:] = (kv[:, HD:] * scale).astype(jnp.bfloat16)


def project_slots(order, slots, weights, text_kv, text_total, cosine, sine):
    rows = text_kv.shape[0]
    slot_count = Z * slots[0].shape[0]
    width = HALF_D + slots[-1].shape[1]
    shape = jax.ShapeDtypeStruct
    return pl.pallas_call(
        slot_kernel,
        in_specs=[SMEM] + [ANY] * (len(slots) + len(weights)) + [VMEM] * 4,
        out_specs=[VMEM, VMEM],
        out_shape=[shape((rows, 2 * HD), jnp.bfloat16), shape((rows, HD), jnp.float32)],
        scratch_shapes=[
            pltpu.VMEM((slot_count, width), jnp.bfloat16),
            pltpu.VMEM((len(SHARDS), (width - AUX) // len(SHARDS), 2 * HD), jnp.bfloat16),
            pltpu.SemaphoreType.DMA((SLOT_COPIES,)),
            pltpu.SemaphoreType.DMA((len(SHARDS),)),
        ],
        compiler_params=pltpu.CompilerParams(vmem_limit_bytes=VMEM_BYTES),
        name="project_slots",
    )(order, *slots, *weights, text_kv, text_total, cosine, sine)


GROUP = 2
SOFT = HD ** (-0.5) * LOG2E
LIMIT = 60.0


def query_kernel(*refs):
    order_ref, text_ref, refs = refs[0], refs[1], refs[2:]
    pieces, refs = refs[:Z + YH], refs[Z + YH:]
    sources, others, refs = refs[:C * ARRAYS], refs[C * ARRAYS:2 * C * ARRAYS], refs[2 * C * ARRAYS:]
    scale_ref, cos_ref, sin_ref, kv_ref, start_ref, q_ref, top_ref, sum_ref, acc_ref = refs[:9]
    slots_ref, weight_ref, total_ref, slot_sems, sems, other_sems = refs[9:]
    rows, width = text_ref.shape
    wide = GROUP * rows
    loads = slot_copies(pieces, slots_ref, slot_sems)
    copies = weight_copies(sources, weight_ref, sems, slice(2 * HD, 2 * HD + SPLIT), 0)
    more = weight_copies(others, weight_ref, other_sems, slice(0, others[0].shape[1]), SPLIT)
    for copy in loads:
        copy.start()
    for copy, other in zip(copies, more):
        copy.start()
        other.start()
    for copy in loads:
        copy.wait()
    marks = slots_ref[:, width:]
    pick = slot_pick(marks, rows)
    held = jnp.dot(pick, marks, preferred_element_type=jnp.float32)[:, 2:3] > 0.5
    depth = weight_ref.shape[1]
    for n, (copy, other) in enumerate(zip(copies, more)):
        copy.wait()
        other.wait()
        part = columns_of(order_ref, n, depth)
        image = jnp.dot(pick, slots_ref[:, part], preferred_element_type=jnp.float32)
        mixed = jnp.where(held, image, text_ref[:, part].astype(jnp.float32)).astype(jnp.bfloat16)
        value = jnp.dot(mixed, weight_ref[n], preferred_element_type=jnp.float32)
        total_ref[...] = value if n == 0 else total_ref[...] + value
    heads = total_ref.shape[1] // HD
    for h in range(heads):
        part = total_ref[:, h * HD:(h + 1) * HD] * scale_ref[...]
        q_ref[h * rows:(h + 1) * rows, :] = turned(part, cos_ref[...], sin_ref[...]).astype(jnp.bfloat16)
    key_at = lax.broadcasted_iota(jnp.int32, (rows, rows), 0)
    query_at = lax.broadcasted_iota(jnp.int32, (rows, rows), 1)
    allowed = (key_at <= query_at) & (key_at >= start_ref[0:1, :])
    allowed = jnp.concatenate([allowed] * GROUP, axis=1)
    for g in range(heads // GROUP):
        part = slice(g * wide, (g + 1) * wide)
        scores = lax.dot_general(
            kv_ref[:, :HD], q_ref[part, :], (((1,), (1,)), ((), ())), preferred_element_type=jnp.float32
        )
        scores = jnp.where(allowed, scores, BIG_NEG)
        top = jnp.max(scores, axis=0, keepdims=True)
        probs = jnp.exp2((scores - top) * SOFT)
        top_ref[:, part] = top
        sum_ref[:, part] = jnp.sum(probs, axis=0, keepdims=True)
        acc_ref[:, part] = lax.dot_general(
            kv_ref[:, HD:], probs.astype(jnp.bfloat16), (((0,), (0,)), ((), ())),
            preferred_element_type=jnp.float32,
        )


def query(order, text_rows, slots, weights, more, scale, cosine, sine, kv, starts, heads):
    rows, width = text_rows.shape
    slot_count = Z * slots[0].shape[0]
    wide = heads * rows
    shape = jax.ShapeDtypeStruct
    return pl.pallas_call(
        query_kernel,
        in_specs=[SMEM, VMEM] + [ANY] * (len(slots) + len(weights) + len(more)) + [VMEM] * 5,
        out_specs=[VMEM] * 4,
        out_shape=[
            shape((wide, HD), jnp.bfloat16),
            shape((1, wide), jnp.float32),
            shape((1, wide), jnp.float32),
            shape((HD, wide), jnp.float32),
        ],
        scratch_shapes=[
            pltpu.VMEM((slot_count, width + AUX), jnp.bfloat16),
            pltpu.VMEM((len(SHARDS), width // len(SHARDS), heads * HD), jnp.bfloat16),
            pltpu.VMEM((rows, heads * HD), jnp.float32),
            pltpu.SemaphoreType.DMA((SLOT_COPIES,)),
            pltpu.SemaphoreType.DMA((len(SHARDS),)),
            pltpu.SemaphoreType.DMA((len(SHARDS),)),
        ],
        compiler_params=pltpu.CompilerParams(vmem_limit_bytes=VMEM_BYTES),
        name="query",
    )(order, text_rows, *slots, *weights, *more, scale, cosine, sine, kv, starts)


def attention_kernel(
    info_ref, q_ref, top_in, sum_in, acc_in, kv_ref, start_ref, out_ref, base_ref, top_ref, sum_ref, acc_ref
):
    rows = out_ref.shape[0]
    heads = out_ref.shape[1] // HD
    wide = GROUP * rows
    me = info_ref[0]
    first = info_ref[1]
    edge = info_ref[2]
    count = me - first

    def allowed_keys(indices):
        masks = []
        for index in indices:
            key_at = (index - me) * rows + lax.broadcasted_iota(jnp.int32, (rows, rows), 0)
            masks.append(key_at >= start_ref[0:1, :])
        return jnp.concatenate([jnp.concatenate(masks, axis=0)] * GROUP, axis=1)

    def loaded(indices):
        keys = jnp.concatenate([kv_ref[index, :, :HD] for index in indices], axis=0)
        values = jnp.concatenate([kv_ref[index, :, HD:] for index in indices], axis=0)
        return keys, values

    def scores_of(keys, part, allowed):
        scores = lax.dot_general(
            keys, q_ref[part, :], (((1,), (1,)), ((), ())), preferred_element_type=jnp.float32
        )
        return scores if allowed is None else jnp.where(allowed, scores, BIG_NEG)

    def mixed_of(values, probs):
        return lax.dot_general(
            values, probs.astype(jnp.bfloat16), (((0,), (0,)), ((), ())), preferred_element_type=jnp.float32
        )

    def fast(indices, masked):
        keys, values = loaded(indices)
        allowed = allowed_keys(indices) if masked else None
        for g in range(heads // GROUP):
            part = slice(g * wide, (g + 1) * wide)
            scores = scores_of(keys, part, allowed)
            top_ref[:, part] = jnp.maximum(top_ref[:, part], jnp.max(scores, axis=0, keepdims=True))
            probs = jnp.exp2(scores * SOFT - base_ref[:, part])
            acc_ref[:, part] += mixed_of(values, probs)
            sum_ref[:, part] += jnp.sum(probs, axis=0, keepdims=True)

    def slow(index):
        keys, values = loaded([index])
        allowed = allowed_keys([index])
        for g in range(heads // GROUP):
            part = slice(g * wide, (g + 1) * wide)
            scores = scores_of(keys, part, allowed)
            old = top_ref[:, part]
            top = jnp.maximum(old, jnp.max(scores, axis=0, keepdims=True))
            probs = jnp.exp2((scores - top) * SOFT)
            shrink = jnp.exp2((old - top) * SOFT)
            top_ref[:, part] = top
            sum_ref[:, part] = sum_ref[:, part] * shrink + jnp.sum(probs, axis=0, keepdims=True)
            acc_ref[:, part] = acc_ref[:, part] * shrink + mixed_of(values, probs)

    def start():
        top_ref[...] = top_in[...]
        sum_ref[...] = sum_in[...]
        acc_ref[...] = acc_in[...]

    def either(indices):
        needs = indices[-1] * rows < edge

        @pl.when(needs)
        def _():
            fast(indices, True)

        @pl.when(jnp.logical_not(needs))
        def _():
            fast(indices, False)

    start()
    base_ref[...] = top_in[...] * SOFT
    odd = count % 2

    @pl.when(odd == 1)
    def _():
        either([me - 1])

    def pair(i, _):
        at = me - 1 - odd - 2 * i
        either([at, at - 1])
        return 0

    lax.fori_loop(0, count // 2, pair, 0)
    grown = jnp.max(top_ref[...] * SOFT - base_ref[...])

    @pl.when(grown > LIMIT)
    def _():
        start()

        def again(i, _):
            slow(me - 1 - i)
            return 0

        lax.fori_loop(0, count, again, 0)

    for h in range(heads):
        part = slice(h * rows, (h + 1) * rows)
        out_ref[:, h * HD:(h + 1) * HD] = (acc_ref[:, part] / sum_ref[:, part]).T.astype(jnp.bfloat16)


def attend(info, state, kv_all, starts):
    rows = kv_all.shape[1]
    wide = state[0].shape[0]
    vmem = pl.BlockSpec(memory_space=pltpu.VMEM)
    return pl.pallas_call(
        attention_kernel,
        in_specs=[pl.BlockSpec(memory_space=pltpu.SMEM)] + [vmem] * 6,
        out_specs=vmem,
        out_shape=jax.ShapeDtypeStruct((rows, wide // rows * HD), jnp.bfloat16),
        scratch_shapes=[
            pltpu.VMEM((1, wide), jnp.float32),
            pltpu.VMEM((1, wide), jnp.float32),
            pltpu.VMEM((1, wide), jnp.float32),
            pltpu.VMEM((HD, wide), jnp.float32),
        ],
        compiler_params=pltpu.CompilerParams(vmem_limit_bytes=VMEM_BYTES),
        name="attend",
    )(info, *state, kv_all, starts)


def per_device(
    patches,
    merge_up,
    merge_down,
    image_pos,
    text_rows,
    segment,
    query_weight,
    key_weight,
    value_weight,
):
    seq_count = lax.axis_size("seq")
    seq_index = lax.axis_index("seq")
    rows, width = text_rows.shape
    bf16, f32 = jnp.bfloat16, jnp.float32

    def after(array, *others):
        return lax.optimization_barrier((array, *others))[0]

    def other_core(arrays):
        return list(arrays) + [seq_shift(array, 0, 0, 1) for array in arrays]

    with jax.named_scope("weights"):
        first = jnp.concatenate([key_weight, value_weight, query_weight[:, :SPLIT]], axis=1)
        second = query_weight[:, SPLIT:]
        first_beside = seq_shift(first, 0, 1, 0)

    with jax.named_scope("merger"):
        up_other = seq_shift(merge_up.T, 0, 0, 1)
        down_other = seq_shift(merge_down, 0, 0, 1)
        merged = prepare(patches, segment)
        own = merged.shape[0]
        near = jnp.concatenate([merged] + [seq_shift(merged, dx, 0, 0) for dx in range(1, X)], axis=0)
        far = seq_shift(near, 0, 1, 0)

    with jax.named_scope("weights"):
        first_pair = jnp.concatenate([first, after(first_beside, near)], axis=0)
        first_up, first_down = seq_shift(first_pair, 1, 0, 0), seq_shift(first_pair, -1, 0, 0)
        second_beside = seq_shift(after(second, far), 0, 1, 0)

    with jax.named_scope("merger"):
        outs = merger(near, far, (merge_up.T, up_other), (merge_down, down_other))
        part_a, part_b = outs[:X], outs[X:]

    with jax.named_scope("sums"):
        got_a = [seq_shift(part_a[dx], -dx, 0, 0) for dx in range(1, X)]
        got_b = seq_shift(part_b[1], 0, 1, 0)
        sum_a = part_a[0] + sum(piece.astype(f32) for piece in got_a)
        sum_b = part_b[0] + got_b.astype(f32)
        last_a = seq_shift(sum_a[own:].astype(bf16), 0, 1, 0)
        last_b = [seq_shift(sum_b[dx * own:(dx + 1) * own].astype(bf16), -dx, 0, 0) for dx in range(1, X)]
        image_a = (sum_a[:own] + last_a.astype(f32)).astype(bf16)
        image_b = (sum_b[:own] + sum(piece.astype(f32) for piece in last_b)).astype(bf16)

    def relayed(up, down):
        depth = up.shape[0] // Y
        return seq_shift(up[:depth], 1, 0, 0), seq_shift(down[depth:], -1, 0, 0)

    with jax.named_scope("weights"):
        first_up, first_down, sum_a, sum_b = lax.optimization_barrier((first_up, first_down, sum_a, sum_b))
        first_weights = other_core([first_pair, first_up, first_down, *relayed(first_up, first_down)])
        second_pair = jnp.concatenate([second, after(second_beside, image_a, image_b)], axis=0)
        second_up, second_down = seq_shift(second_pair, 1, 0, 0), seq_shift(second_pair, -1, 0, 0)

    with jax.named_scope("segments"):
        counted = sum(
            block[at:at + 1, merge_up.shape[0]:].astype(f32)
            for block in (near, far)
            for at in range(0, X * own, own)
        )
        counted = (counted + seq_shift(counted, 0, 0, 1))[0]
        ends = (counted[:3] * 128.0 + counted[3:6]).astype(jnp.int32)
        before = jnp.concatenate([jnp.zeros((1,), jnp.int32), ends])
        starts = jnp.sum(
            jnp.where(segment[None, :] == jnp.arange(4, dtype=jnp.int32)[:, None], before[:, None], 0), axis=0
        )
        info = jnp.stack([seq_index, starts[0] // rows, starts[-1]]).astype(jnp.int32)
        starts = (starts - seq_index * rows)[None, :]

    with jax.named_scope("angles"):
        positions = (seq_index * rows + jnp.arange(rows, dtype=jnp.int32)).astype(f32)
        frequency = ROPE_BASE ** (-(jnp.arange(HD // 2, dtype=f32) * 2.0 / HD))
        angles = positions[:, None] * frequency[None, :]
        cosine, sine = jnp.cos(angles), jnp.sin(angles)
        cosine = jnp.concatenate([cosine, cosine], axis=1)
        sine = jnp.concatenate([-sine, sine], axis=1)

    with jax.named_scope("route"):
        target = image_pos // rows
        offset = image_pos % rows
        matches = (target[:, None] == jnp.arange(seq_count, dtype=jnp.int32)[None, :]).astype(jnp.int32)
        slot_rank = jnp.sum((jnp.cumsum(matches, axis=0) - matches) * matches, axis=1)
        slot_index = target * CAP + slot_rank
        select = (slot_index[None, :] == jnp.arange(seq_count * CAP, dtype=jnp.int32)[:, None]).astype(bf16)
        marks = jnp.stack([offset // 128, offset % 128, jnp.ones_like(offset)], axis=1).astype(bf16)
        marks = jnp.pad(marks, ((0, 0), (0, AUX - 3)))
        send = jnp.dot(
            select, jnp.concatenate([image_a, image_b, marks], axis=1), preferred_element_type=f32
        ).astype(bf16)
        got = lax.all_to_all(
            send.reshape(seq_count, CAP, width + AUX), "seq", split_axis=0, concat_axis=0, tiled=True
        ).reshape(seq_count * CAP, width + AUX)
        got, info, starts, cosine, sine = lax.optimization_barrier((got, info, starts, cosine, sine))
        got_a, got_b = got[:, :HALF_D], got[:, HALF_D:]
        pair_a = jnp.concatenate([got_a, pool_shift(got_a, 0, 1)], axis=0)
        column_b = jnp.concatenate([got_b] + [pool_shift(got_b, dz, 0) for dz in range(1, Z)], axis=0)
        slots = [pair_a] + [pool_shift(pair_a, dz, 0) for dz in range(1, Z)]
        slots += [column_b, pool_shift(column_b, 0, 1)]

    with jax.named_scope("weights"):
        second_up, second_down, text_here = lax.optimization_barrier(
            (second_up, second_down, text_rows, pair_a, column_b)
        )[:3]
        second_weights = other_core([second_pair, second_up, second_down, *relayed(second_up, second_down)])

    with jax.named_scope("project"):
        x_at, y_at, c_at = seq_index // (Y * C), seq_index // C % Y, seq_index % C
        order = jnp.stack(
            [(x_at + dx) % X * (Y * C) + (y_at ^ dy) * C + (c_at ^ dc) for _, _, dx, dy, dc in SHARDS]
        ).astype(jnp.int32)
        text_kv, text_total = project_text(order, text_here, first_weights)
        kv, scale = project_slots(order, slots, first_weights, text_kv, text_total, cosine, sine)
        kv_all = lax.all_gather(kv, "seq", axis=0, tiled=True)
        state = query(
            order, text_rows, slots, first_weights, second_weights, scale, cosine, sine, kv, starts,
            query_weight.shape[1] // HD,
        )

    with jax.named_scope("attend"):
        return attend(info, state, kv_all.reshape(seq_count, rows, 2 * HD), starts)


def solution(mesh):
    return jax.shard_map(
        per_device,
        mesh=mesh,
        in_specs=(
            P(("pool", "seq"), None),
            P(None, "seq"),
            P("seq", None),
            P(("pool", "seq")),
            P("seq", None),
            P("seq"),
            P("seq", "pool"),
            P("seq", "pool"),
            P("seq", "pool"),
        ),
        out_specs=P("seq", "pool"),
        check_vma=False,
    )
```

```python
import jax
import jax.numpy as jnp
from jax import lax
from jax.experimental import pallas as pl
from jax.experimental.pallas import tpu as pltpu
from jax.sharding import PartitionSpec as P

HD = 128
CAP = 2
AUX = 128
NORM_EPS = 1e-06
ROPE_BASE = 1000000.0
BIG_NEG = -1e30
LOG2E = 1.4426950408889634
VMEM_BYTES = 56 * 1024 * 1024
X, Y, C = 4, 2, 2
Z, YH = 4, 2
CHUNK = 1024
SLOT_CHUNK = 4096
SEQ, POOL = "seq", "pool"


def rms_rows(matrix):
    return matrix * lax.rsqrt(jnp.mean(matrix * matrix, axis=-1, keepdims=True) + NORM_EPS)


def seq_shift(array, dx, dy, dc):
    pairs = []
    for source in range(X * Y * C):
        x, y, c = source // (Y * C), source // C % Y, source % C
        pairs.append((source, ((x + dx) % X) * Y * C + (y ^ dy) * C + (c ^ dc)))
    return lax.ppermute(array, SEQ, pairs)


SUM_SPLIT = 4096
POOL_SPLIT = 4096


def pool_shift(array, dz, dy):
    pairs = []
    for source in range(Z * YH):
        z, y = source // YH, source % YH
        pairs.append((source, ((z + dz) % Z) * YH + (y ^ dy)))
    return lax.ppermute(array, POOL, pairs)


def whole(shape):
    return pl.BlockSpec(shape, lambda n: (0, 0), pipeline_mode=pl.Buffered(1))


def patch_kernel(patches_ref, segment_ref, out_ref):
    own = out_ref.shape[0]
    patch_count, width = patches_ref.shape
    normed = rms_rows(patches_ref[...].astype(jnp.float32)).astype(jnp.bfloat16)
    token = lax.broadcasted_iota(jnp.int32, (own, patch_count), 0)
    patch = lax.broadcasted_iota(jnp.int32, (own, patch_count), 1)
    for k in range(4):
        pick = jnp.where(patch == 4 * token + k, 1.0, 0.0).astype(jnp.bfloat16)
        out_ref[:, k * width:(k + 1) * width] = jnp.dot(
            pick, normed, preferred_element_type=jnp.float32
        ).astype(jnp.bfloat16)
    lane = lax.broadcasted_iota(jnp.int32, (own, AUX), 1)
    marks = jnp.zeros((own, AUX), jnp.float32)
    for v in range(1, 4):
        before = jnp.sum(jnp.where(segment_ref[...] < v, 1.0, 0.0), axis=1, keepdims=True)
        high = jnp.floor(before * (1.0 / 128.0))
        marks += jnp.where(lane == v - 1, high, 0.0) + jnp.where(lane == v + 2, before - 128.0 * high, 0.0)
    out_ref[:, 4 * width:] = marks.astype(jnp.bfloat16)


def prepare(patches, segment):
    vmem = pl.BlockSpec(memory_space=pltpu.VMEM)
    return pl.pallas_call(
        patch_kernel,
        in_specs=[vmem, vmem],
        out_specs=vmem,
        out_shape=jax.ShapeDtypeStruct((patches.shape[0] // 4, 4 * patches.shape[1] + AUX), jnp.bfloat16),
        name="prepare",
    )(patches, segment[None, :])


ANY = pl.BlockSpec(memory_space=pl.ANY)
VMEM = pl.BlockSpec(memory_space=pltpu.VMEM)
SMEM = pl.BlockSpec(memory_space=pltpu.SMEM)


def merger_kernel(*refs):
    pieces, (up_a, up_b, down_a, down_b), refs = refs[:X], refs[X:X + 4], refs[X + 4:]
    outs, (up_ref, down_ref, sems) = refs[:X + Y], refs[X + Y:]
    units, depth = up_a.shape
    own = pieces[0].shape[0] // Y
    halves = [slice(0, SUM_SPLIT), slice(SUM_SPLIT, down_a.shape[1])]
    copies = []
    for at, source in enumerate((up_a, up_b)):
        copies.append(pltpu.make_async_copy(source, up_ref.at[pl.ds(at * units, units), :], sems.at[at]))
    for n, half in enumerate(halves):
        for at, source in enumerate((down_a, down_b)):
            copies.append(
                pltpu.make_async_copy(
                    source.at[:, half], down_ref.at[pl.ds(at * units, units), half], sems.at[2 + 2 * n + at]
                )
            )
    for copy in copies:
        copy.start()
    merged = jnp.concatenate([piece[:, :depth] for piece in pieces], axis=0)
    hidden = []
    for at in range(2):
        copies[at].wait()
        value = lax.dot_general(
            merged, up_ref[at * units:(at + 1) * units, :], (((1,), (1,)), ((), ())),
            preferred_element_type=jnp.float32,
        )
        hidden.append((0.5 * value * (1.0 + lax.erf(value * (0.5 ** 0.5)))).astype(jnp.bfloat16))
    hidden = jnp.concatenate(hidden, axis=1)
    for n, half in enumerate(halves):
        copies[2 + 2 * n].wait()
        copies[3 + 2 * n].wait()
        for start in range(half.start, half.stop, CHUNK):
            total = jnp.dot(hidden, down_ref[:, start:start + CHUNK], preferred_element_type=jnp.float32)
            part = slice(start - half.start, start - half.start + CHUNK)
            if n == 0:
                for dx in range(X):
                    at = dx * Y * own
                    outs[dx][:, part] = total[at:at + Y * own].astype(outs[dx].dtype)
            else:
                for dx in range(X):
                    for dy in range(Y):
                        at = (dx * Y + dy) * own
                        outs[X + dy][dx * own:(dx + 1) * own, part] = total[at:at + own].astype(outs[X + dy].dtype)


def merger(pieces, ups, downs):
    units, depth = ups[0].shape
    width = downs[0].shape[1]
    own = pieces[0].shape[0] // Y
    shape = jax.ShapeDtypeStruct
    return pl.pallas_call(
        merger_kernel,
        in_specs=[VMEM] * X + [ANY] * 4,
        out_specs=[VMEM] * (X + Y),
        out_shape=[shape((Y * own, SUM_SPLIT), jnp.float32 if dx == 0 else jnp.bfloat16) for dx in range(X)]
        + [shape((X * own, width - SUM_SPLIT), jnp.float32 if dy == 0 else jnp.bfloat16) for dy in range(Y)],
        scratch_shapes=[
            pltpu.VMEM((2 * units, depth), jnp.bfloat16),
            pltpu.VMEM((2 * units, width), jnp.bfloat16),
            pltpu.SemaphoreType.DMA((6,)),
        ],
        compiler_params=pltpu.CompilerParams(vmem_limit_bytes=VMEM_BYTES),
        name="merger",
    )(*pieces, *ups, *downs)


def turned(part, cosine, sine):
    return part * cosine + pltpu.roll(part, HD // 2, 1) * sine


def slot_marks(b0, b1):
    cap = b0.shape[0] // Z
    at = b0.shape[1] - AUX
    blocks = []
    for dz in range(Z):
        for ref in (b0, b1):
            blocks.append(ref[dz * cap:(dz + 1) * cap, at:])
    return jnp.concatenate(blocks, axis=0), jnp.concatenate([b0[:, at:], b1[:, at:]], axis=0)


def slot_pick(marks, rows):
    value = marks.astype(jnp.float32)
    offset = value[:, 0:1] * 128.0 + value[:, 1:2]
    offset = jnp.where(value[:, 2:3] > 0.5, offset, -1.0).astype(jnp.int32)
    token = lax.broadcasted_iota(jnp.int32, (value.shape[0], rows), 1)
    return jnp.where(offset == token, 1.0, 0.0).T.astype(jnp.bfloat16)


def lane_sums(matrix):
    total = matrix[:, :HD]
    for at in range(HD, matrix.shape[1], HD):
        total += matrix[:, at:at + HD]
    return total


KV_BLOCK = 4


def slot_columns(refs, n, chunk):
    part = pl.ds(pl.multiple_of(n * chunk, chunk), chunk)
    return jnp.concatenate([ref[:, part] for ref in refs], axis=0)


def text_kernel(text_ref, weight_ref, kv_ref, total_ref):
    @pl.when(pl.program_id(0) == 0)
    def _():
        kv_ref[...] = jnp.zeros_like(kv_ref)
        total_ref[...] = jnp.zeros_like(total_ref)

    kv_ref[...] += jnp.dot(text_ref[...], weight_ref[...], preferred_element_type=jnp.float32)
    value = text_ref[...].astype(jnp.float32)
    total_ref[...] += lane_sums(value * value)


def project_text(text_rows, weights):
    rows, width = text_rows.shape
    kv_block = weights.shape[1] // (2 * HD) - 1
    shape = jax.ShapeDtypeStruct
    return pl.pallas_call(
        text_kernel,
        grid=(width // CHUNK,),
        in_specs=[
            pl.BlockSpec((rows, CHUNK), lambda n: (0, n)),
            pl.BlockSpec((CHUNK, 2 * HD), lambda n: (n, kv_block)),
        ],
        out_specs=[whole((rows, 2 * HD)), whole((rows, HD))],
        out_shape=[shape((rows, 2 * HD), jnp.float32), shape((rows, HD), jnp.float32)],
        compiler_params=pltpu.CompilerParams(vmem_limit_bytes=VMEM_BYTES),
        name="project_text",
    )(text_rows, weights)


def slot_kernel(
    a0, a1, a2, a3, b0, b1, weight_ref, text_kv_ref, text_total_ref, cos_ref, sin_ref,
    kv_ref, scale_ref, sum_ref, total_ref,
):
    rows = text_kv_ref.shape[0]
    step = pl.program_id(0)
    steps = pl.num_programs(0)
    half = POOL_SPLIT // SLOT_CHUNK
    width = steps * SLOT_CHUNK

    @pl.when(step == 0)
    def _():
        sum_ref[...] = jnp.zeros_like(sum_ref)
        total_ref[...] = jnp.zeros_like(total_ref)

    def add(at, refs, index):
        slots = slot_columns(refs, index, SLOT_CHUNK)
        sum_ref[at] += jnp.dot(slots, weight_ref[...], preferred_element_type=jnp.float32)
        value = slots.astype(jnp.float32)
        total_ref[at] += lane_sums(value * value)

    @pl.when(step < half)
    def _():
        add(0, (a0, a1, a2, a3), step)

    @pl.when(step >= half)
    def _():
        add(1, (b0, b1), step - half)

    @pl.when(step == steps - 1)
    def _():
        marks = slot_marks(b0, b1)[1]
        pick = slot_pick(marks, rows)
        held = jnp.dot(pick, marks, preferred_element_type=jnp.float32)[:, 2:3] > 0.5
        cap = marks.shape[0] // (Z * YH)

        def joined(ref):
            first = [
                ref[0, (dz * YH + yh) * cap:(dz * YH + yh + 1) * cap, :] for yh in range(YH) for dz in range(Z)
            ]
            return jnp.concatenate(first, axis=0) + ref[1]

        def placed(value):
            high = value.astype(jnp.bfloat16)
            low = (value - high.astype(jnp.float32)).astype(jnp.bfloat16)
            return jnp.dot(pick, high, preferred_element_type=jnp.float32) + jnp.dot(
                pick, low, preferred_element_type=jnp.float32
            )

        def scale_of(total):
            return lax.rsqrt(jnp.sum(total, axis=1, keepdims=True) / width + NORM_EPS)

        slot_scale = scale_of(joined(total_ref))
        text_scale = scale_of(text_total_ref[...])
        slot_scale = jnp.broadcast_to(slot_scale, (slot_scale.shape[0], HD))
        scale = jnp.where(held, placed(slot_scale), text_scale)
        scale_ref[...] = scale
        kv = jnp.where(held, placed(joined(sum_ref)), text_kv_ref[...])
        kv_ref[:, :HD] = turned(kv[:, :HD] * scale, cos_ref[...], sin_ref[...]).astype(jnp.bfloat16)
        kv_ref[:, HD:] = (kv[:, HD:] * scale).astype(jnp.bfloat16)


def project_slots(slots_a, slots_b, weights, text_kv, text_total, cosine, sine):
    rows = text_kv.shape[0]
    width = weights.shape[0]
    slot_count = X * slots_a[0].shape[0]
    kv_block = weights.shape[1] // (2 * HD) - 1
    shape = jax.ShapeDtypeStruct
    return pl.pallas_call(
        slot_kernel,
        grid=(width // SLOT_CHUNK,),
        in_specs=[whole(piece.shape) for piece in slots_a]
        + [whole(piece.shape) for piece in slots_b]
        + [pl.BlockSpec((SLOT_CHUNK, 2 * HD), lambda n: (n, kv_block))]
        + [whole((rows, 2 * HD)), whole((rows, HD)), whole((rows, HD)), whole((rows, HD))],
        out_specs=[whole((rows, 2 * HD)), whole((rows, HD))],
        out_shape=[shape((rows, 2 * HD), jnp.bfloat16), shape((rows, HD), jnp.float32)],
        scratch_shapes=[
            pltpu.VMEM((2, slot_count, 2 * HD), jnp.float32),
            pltpu.VMEM((2, slot_count, HD), jnp.float32),
        ],
        compiler_params=pltpu.CompilerParams(vmem_limit_bytes=VMEM_BYTES),
        name="project_slots",
    )(*slots_a, *slots_b, weights, text_kv, text_total, cosine, sine)


GROUP = 2
SOFT = HD ** (-0.5) * LOG2E
LIMIT = 60.0
STEP = 4


def query_kernel(
    text_ref, a0, a1, a2, a3, b0, b1, weight_ref, scale_ref, cos_ref, sin_ref, kv_ref, start_ref,
    q_ref, top_ref, sum_ref, acc_ref, pick_a, pick_b, held_ref, total_ref,
):
    rows = text_ref.shape[0]
    step = pl.program_id(0)
    steps = pl.num_programs(0)
    half = POOL_SPLIT // CHUNK
    wide = GROUP * rows

    @pl.when(step == 0)
    def _():
        marks_a, marks_b = slot_marks(b0, b1)
        pick_a[...] = slot_pick(marks_a, rows)
        pick_b[...] = slot_pick(marks_b, rows)
        held_ref[...] = jnp.dot(pick_b[...], marks_b, preferred_element_type=jnp.float32)
        total_ref[...] = jnp.zeros_like(total_ref)

    def add(pick, refs, index):
        slots = slot_columns(refs, index, CHUNK)
        image = jnp.dot(pick[...], slots, preferred_element_type=jnp.float32)
        mixed = jnp.where(held_ref[:, 2:3] > 0.5, image, text_ref[...].astype(jnp.float32)).astype(jnp.bfloat16)
        total_ref[...] += jnp.dot(mixed, weight_ref[...], preferred_element_type=jnp.float32)

    @pl.when(step < half)
    def _():
        add(pick_a, (a0, a1, a2, a3), step)

    @pl.when(step >= half)
    def _():
        add(pick_b, (b0, b1), step - half)

    @pl.when(step == steps - 1)
    def _():
        heads = total_ref.shape[1] // HD
        for h in range(heads):
            part = total_ref[:, h * HD:(h + 1) * HD] * scale_ref[...]
            q_ref[h * rows:(h + 1) * rows, :] = turned(part, cos_ref[...], sin_ref[...]).astype(jnp.bfloat16)
        key_at = lax.broadcasted_iota(jnp.int32, (rows, rows), 0)
        query_at = lax.broadcasted_iota(jnp.int32, (rows, rows), 1)
        allowed = (key_at <= query_at) & (key_at >= start_ref[0:1, :])
        allowed = jnp.concatenate([allowed] * GROUP, axis=1)
        for g in range(heads // GROUP):
            part = slice(g * wide, (g + 1) * wide)
            scores = lax.dot_general(
                kv_ref[:, :HD], q_ref[part, :], (((1,), (1,)), ((), ())), preferred_element_type=jnp.float32
            )
            scores = jnp.where(allowed, scores, BIG_NEG)
            top = jnp.max(scores, axis=0, keepdims=True)
            probs = jnp.exp2((scores - top) * SOFT)
            top_ref[:, part] = top
            sum_ref[:, part] = jnp.sum(probs, axis=0, keepdims=True)
            acc_ref[:, part] = lax.dot_general(
                kv_ref[:, HD:], probs.astype(jnp.bfloat16), (((0,), (0,)), ((), ())),
                preferred_element_type=jnp.float32,
            )


def query(text_rows, slots_a, slots_b, weights, scale, cosine, sine, kv, starts, heads):
    rows, width = text_rows.shape
    slot_count = X * slots_a[0].shape[0]
    wide = heads * rows
    shape = jax.ShapeDtypeStruct
    return pl.pallas_call(
        query_kernel,
        grid=(width // CHUNK,),
        in_specs=[pl.BlockSpec((rows, CHUNK), lambda n: (0, n))]
        + [whole(piece.shape) for piece in slots_a]
        + [whole(piece.shape) for piece in slots_b]
        + [pl.BlockSpec((CHUNK, heads * HD), lambda n: (n, 0))]
        + [whole((rows, HD))] * 3
        + [whole((rows, 2 * HD)), whole((1, rows))],
        out_specs=[whole((wide, HD)), whole((1, wide)), whole((1, wide)), whole((HD, wide))],
        out_shape=[
            shape((wide, HD), jnp.bfloat16),
            shape((1, wide), jnp.float32),
            shape((1, wide), jnp.float32),
            shape((HD, wide), jnp.float32),
        ],
        scratch_shapes=[
            pltpu.VMEM((rows, slot_count), jnp.bfloat16),
            pltpu.VMEM((rows, slot_count), jnp.bfloat16),
            pltpu.VMEM((rows, AUX), jnp.float32),
            pltpu.VMEM((rows, heads * HD), jnp.float32),
        ],
        compiler_params=pltpu.CompilerParams(vmem_limit_bytes=VMEM_BYTES),
        name="query",
    )(text_rows, *slots_a, *slots_b, weights, scale, cosine, sine, kv, starts)


def attention_kernel(
    info_ref, q_ref, top_in, sum_in, acc_in, kv_ref, start_ref, out_ref, base_ref, top_ref, sum_ref, acc_ref
):
    rows = out_ref.shape[0]
    heads = out_ref.shape[1] // HD
    wide = GROUP * rows
    me = info_ref[0]
    first = info_ref[1]
    clear = info_ref[2]
    count = me - first

    def allowed_keys(indices):
        masks = []
        for index in indices:
            key_at = (index - me) * rows + lax.broadcasted_iota(jnp.int32, (rows, rows), 0)
            masks.append(key_at >= start_ref[0:1, :])
        return jnp.concatenate([jnp.concatenate(masks, axis=0)] * GROUP, axis=1)

    def loaded(indices):
        keys = jnp.concatenate([kv_ref[index, :, :HD] for index in indices], axis=0)
        values = jnp.concatenate([kv_ref[index, :, HD:] for index in indices], axis=0)
        return keys, values

    def scores_of(keys, part, allowed):
        scores = lax.dot_general(
            keys, q_ref[part, :], (((1,), (1,)), ((), ())), preferred_element_type=jnp.float32
        )
        return scores if allowed is None else jnp.where(allowed, scores, BIG_NEG)

    def mixed_of(values, probs):
        return lax.dot_general(
            values, probs.astype(jnp.bfloat16), (((0,), (0,)), ((), ())), preferred_element_type=jnp.float32
        )

    def fast(indices, masked):
        keys, values = loaded(indices)
        allowed = allowed_keys(indices) if masked else None
        for g in range(heads // GROUP):
            part = slice(g * wide, (g + 1) * wide)
            scores = scores_of(keys, part, allowed)
            top_ref[:, part] = jnp.maximum(top_ref[:, part], jnp.max(scores, axis=0, keepdims=True))
            probs = jnp.exp2(scores * SOFT - base_ref[:, part])
            acc_ref[:, part] += mixed_of(values, probs)
            sum_ref[:, part] += jnp.sum(probs, axis=0, keepdims=True)

    def slow(index):
        keys, values = loaded([index])
        allowed = allowed_keys([index])
        for g in range(heads // GROUP):
            part = slice(g * wide, (g + 1) * wide)
            scores = scores_of(keys, part, allowed)
            old = top_ref[:, part]
            top = jnp.maximum(old, jnp.max(scores, axis=0, keepdims=True))
            probs = jnp.exp2((scores - top) * SOFT)
            shrink = jnp.exp2((old - top) * SOFT)
            top_ref[:, part] = top
            sum_ref[:, part] = sum_ref[:, part] * shrink + jnp.sum(probs, axis=0, keepdims=True)
            acc_ref[:, part] = acc_ref[:, part] * shrink + mixed_of(values, probs)

    def start():
        top_ref[...] = top_in[...]
        sum_ref[...] = sum_in[...]
        acc_ref[...] = acc_in[...]

    start()
    base_ref[...] = top_in[...] * SOFT
    plain = me - clear

    def step(i, _):
        at = me - 1 - STEP * i
        fast([at - n for n in range(STEP)], False)
        return 0

    lax.fori_loop(0, plain // STEP, step, 0)
    left = plain % STEP

    @pl.when(left >= 2)
    def _():
        fast([clear + left - 1, clear + left - 2], False)

    @pl.when(left % 2 == 1)
    def _():
        fast([clear], False)

    def masked_step(i, _):
        fast([clear - 1 - i], True)
        return 0

    lax.fori_loop(0, clear - first, masked_step, 0)
    grown = jnp.max(top_ref[...] * SOFT - base_ref[...])

    @pl.when(grown > LIMIT)
    def _():
        start()

        def again(i, _):
            slow(me - 1 - i)
            return 0

        lax.fori_loop(0, count, again, 0)

    for h in range(heads):
        part = slice(h * rows, (h + 1) * rows)
        out_ref[:, h * HD:(h + 1) * HD] = (acc_ref[:, part] / sum_ref[:, part]).T.astype(jnp.bfloat16)


def attend(info, state, kv_all, starts):
    rows = kv_all.shape[1]
    wide = state[0].shape[0]
    vmem = pl.BlockSpec(memory_space=pltpu.VMEM)
    return pl.pallas_call(
        attention_kernel,
        in_specs=[pl.BlockSpec(memory_space=pltpu.SMEM)] + [vmem] * 6,
        out_specs=vmem,
        out_shape=jax.ShapeDtypeStruct((rows, wide // rows * HD), jnp.bfloat16),
        scratch_shapes=[
            pltpu.VMEM((1, wide), jnp.float32),
            pltpu.VMEM((1, wide), jnp.float32),
            pltpu.VMEM((1, wide), jnp.float32),
            pltpu.VMEM((HD, wide), jnp.float32),
        ],
        compiler_params=pltpu.CompilerParams(vmem_limit_bytes=VMEM_BYTES),
        name="attend",
    )(info, *state, kv_all, starts)


def per_device(
    patches,
    merge_up,
    merge_down,
    image_pos,
    text_rows,
    segment,
    query_weight,
    key_weight,
    value_weight,
):
    seq_count = lax.axis_size(SEQ)
    seq_index = lax.axis_index(SEQ)
    rows, width = text_rows.shape
    bf16, f32 = jnp.bfloat16, jnp.float32

    def after(array, *others):
        return lax.optimization_barrier((array, *others))[0]

    with jax.named_scope("merger"):
        merged = prepare(patches, segment)
        own = merged.shape[0]
        merged_beside = seq_shift(merged, 0, 1, 0)
        own_weights = jnp.concatenate(
            after((query_weight, key_weight, value_weight), merged_beside), axis=1
        )
        weights = lax.all_gather(own_weights, SEQ, axis=0, tiled=True)
        up_other = seq_shift(merge_up.T, 0, 0, 1)
        down_other = seq_shift(merge_down, 0, 0, 1)
        pair = jnp.concatenate([merged, merged_beside], axis=0)
        pieces = [pair] + [seq_shift(pair, dx, 0, 0) for dx in range(1, X)]
        outs = merger(pieces, (merge_up.T, up_other), (merge_down, down_other))
        part_a, part_b = outs[:X], outs[X:]

    with jax.named_scope("sums"):
        got_a = [seq_shift(part_a[dx], -dx, 0, 0) for dx in range(1, X)]
        got_b = seq_shift(part_b[1], 0, 1, 0)
        sum_a = part_a[0] + sum(piece.astype(f32) for piece in got_a)
        sum_b = part_b[0] + got_b.astype(f32)
        last_a = seq_shift(sum_a[own:].astype(bf16), 0, 1, 0)
        last_b = [seq_shift(sum_b[dx * own:(dx + 1) * own].astype(bf16), -dx, 0, 0) for dx in range(1, X)]
        image_a = (sum_a[:own] + last_a.astype(f32)).astype(bf16)
        image_b = (sum_b[:own] + sum(piece.astype(f32) for piece in last_b)).astype(bf16)

    with jax.named_scope("segments"):
        counted = sum(
            block[at:at + 1, merge_up.shape[0]:].astype(f32)
            for block in pieces
            for at in range(0, Y * own, own)
        )
        counted = (counted + seq_shift(counted, 0, 0, 1))[0]
        ends = (counted[:3] * 128.0 + counted[3:6]).astype(jnp.int32)
        before = jnp.concatenate([jnp.zeros((1,), jnp.int32), ends])
        starts = jnp.sum(
            jnp.where(segment[None, :] == jnp.arange(4, dtype=jnp.int32)[:, None], before[:, None], 0), axis=0
        )
        clear = jnp.minimum((starts[-1] + rows - 1) // rows, seq_index)
        info = jnp.stack([seq_index, starts[0] // rows, clear]).astype(jnp.int32)
        starts = (starts - seq_index * rows)[None, :]

    with jax.named_scope("angles"):
        positions = (seq_index * rows + jnp.arange(rows, dtype=jnp.int32)).astype(f32)
        frequency = ROPE_BASE ** (-(jnp.arange(HD // 2, dtype=f32) * 2.0 / HD))
        angles = positions[:, None] * frequency[None, :]
        cosine, sine = jnp.cos(angles), jnp.sin(angles)
        cosine = jnp.concatenate([cosine, cosine], axis=1)
        sine = jnp.concatenate([-sine, sine], axis=1)

    with jax.named_scope("route"):
        target = image_pos // rows
        offset = image_pos % rows
        matches = (target[:, None] == jnp.arange(seq_count, dtype=jnp.int32)[None, :]).astype(jnp.int32)
        slot_rank = jnp.sum((jnp.cumsum(matches, axis=0) - matches) * matches, axis=1)
        slot_index = target * CAP + slot_rank
        select = (slot_index[None, :] == jnp.arange(seq_count * CAP, dtype=jnp.int32)[:, None]).astype(bf16)
        marks = jnp.stack([offset // 128, offset % 128, jnp.ones_like(offset)], axis=1).astype(bf16)
        marks = jnp.pad(marks, ((0, 0), (0, AUX - 3)))
        send = jnp.dot(
            select, jnp.concatenate([image_a, image_b, marks], axis=1), preferred_element_type=f32
        ).astype(bf16)
        got = lax.all_to_all(
            send.reshape(seq_count, CAP, width + AUX), SEQ, split_axis=0, concat_axis=0, tiled=True
        ).reshape(seq_count * CAP, width + AUX)
        got, info, starts, cosine, sine = lax.optimization_barrier((got, info, starts, cosine, sine))
        got_a, got_b = got[:, :POOL_SPLIT], got[:, POOL_SPLIT:]
        pair_a = jnp.concatenate([got_a, pool_shift(got_a, 0, 1)], axis=0)
        column_b = jnp.concatenate([got_b] + [pool_shift(got_b, dz, 0) for dz in range(1, Z)], axis=0)
        pair_a, column_b, text_here = lax.optimization_barrier((pair_a, column_b, text_rows))
        slots_a = [pair_a] + [pool_shift(pair_a, dz, 0) for dz in range(1, Z)]
        slots_b = [column_b, pool_shift(column_b, 0, 1)]

    with jax.named_scope("project"):
        text_kv, text_total = project_text(text_here, weights)
        kv, scale = project_slots(slots_a, slots_b, weights, text_kv, text_total, cosine, sine)
        kv_all = lax.all_gather(kv, SEQ, axis=0, tiled=True)
        state = query(
            text_rows, slots_a, slots_b, weights, scale, cosine, sine, kv, starts, query_weight.shape[1] // HD
        )

    with jax.named_scope("attend"):
        return attend(info, state, kv_all.reshape(seq_count, rows, 2 * HD), starts)


def solution(mesh):
    return jax.shard_map(
        per_device,
        mesh=mesh,
        in_specs=(
            P(("pool", "seq"), None),
            P(None, "seq"),
            P("seq", None),
            P(("pool", "seq")),
            P("seq", None),
            P("seq"),
            P("seq", "pool"),
            P("seq", "pool"),
            P("seq", "pool"),
        ),
        out_specs=P("seq", "pool"),
        check_vma=False,
    )
```

```python
import jax
import jax.numpy as jnp
from jax import lax
from jax.experimental import pallas as pl
from jax.experimental.pallas import tpu as pltpu
from jax.sharding import PartitionSpec as P

HD = 128
CAP = 2
AUX = 128
NORM_EPS = 1e-06
ROPE_BASE = 1000000.0
BIG_NEG = -1e30
LOG2E = 1.4426950408889634
VMEM_BYTES = 56 * 1024 * 1024
X, Y, C = 4, 2, 2
Z, YH = 4, 2
CHUNK = 1024
SLOT_CHUNK = 4096
SEQ, POOL = "seq", "pool"


def rms_rows(matrix):
    return matrix * lax.rsqrt(jnp.mean(matrix * matrix, axis=-1, keepdims=True) + NORM_EPS)


def seq_shift(array, dx, dy, dc):
    pairs = []
    for source in range(X * Y * C):
        x, y, c = source // (Y * C), source // C % Y, source % C
        pairs.append((source, ((x + dx) % X) * Y * C + (y ^ dy) * C + (c ^ dc)))
    return lax.ppermute(array, SEQ, pairs)


SUM_SPLIT = 4096
POOL_SPLIT = 4096


def pool_shift(array, dz, dy):
    pairs = []
    for source in range(Z * YH):
        z, y = source // YH, source % YH
        pairs.append((source, ((z + dz) % Z) * YH + (y ^ dy)))
    return lax.ppermute(array, POOL, pairs)


def whole(shape):
    return pl.BlockSpec(shape, lambda n: (0, 0), pipeline_mode=pl.Buffered(1))


def patch_kernel(patches_ref, segment_ref, out_ref):
    own = out_ref.shape[0]
    patch_count, width = patches_ref.shape
    normed = rms_rows(patches_ref[...].astype(jnp.float32)).astype(jnp.bfloat16)
    token = lax.broadcasted_iota(jnp.int32, (own, patch_count), 0)
    patch = lax.broadcasted_iota(jnp.int32, (own, patch_count), 1)
    for k in range(4):
        pick = jnp.where(patch == 4 * token + k, 1.0, 0.0).astype(jnp.bfloat16)
        out_ref[:, k * width:(k + 1) * width] = jnp.dot(
            pick, normed, preferred_element_type=jnp.float32
        ).astype(jnp.bfloat16)
    lane = lax.broadcasted_iota(jnp.int32, (own, AUX), 1)
    marks = jnp.zeros((own, AUX), jnp.float32)
    for v in range(1, 4):
        before = jnp.sum(jnp.where(segment_ref[...] < v, 1.0, 0.0), axis=1, keepdims=True)
        high = jnp.floor(before * (1.0 / 128.0))
        marks += jnp.where(lane == v - 1, high, 0.0) + jnp.where(lane == v + 2, before - 128.0 * high, 0.0)
    out_ref[:, 4 * width:] = marks.astype(jnp.bfloat16)


def prepare(patches, segment):
    vmem = pl.BlockSpec(memory_space=pltpu.VMEM)
    return pl.pallas_call(
        patch_kernel,
        in_specs=[vmem, vmem],
        out_specs=vmem,
        out_shape=jax.ShapeDtypeStruct((patches.shape[0] // 4, 4 * patches.shape[1] + AUX), jnp.bfloat16),
        name="prepare",
    )(patches, segment[None, :])


ANY = pl.BlockSpec(memory_space=pl.ANY)
VMEM = pl.BlockSpec(memory_space=pltpu.VMEM)
SMEM = pl.BlockSpec(memory_space=pltpu.SMEM)


def merger_kernel(*refs):
    pieces, (up_a, up_b, down_a, down_b), refs = refs[:X], refs[X:X + 4], refs[X + 4:]
    outs, (up_ref, down_ref, sems) = refs[:X + Y], refs[X + Y:]
    units, depth = up_a.shape
    own = pieces[0].shape[0] // Y
    halves = [slice(0, SUM_SPLIT), slice(SUM_SPLIT, down_a.shape[1])]
    copies = []
    for at, source in enumerate((up_a, up_b)):
        copies.append(pltpu.make_async_copy(source, up_ref.at[pl.ds(at * units, units), :], sems.at[at]))
    for n, half in enumerate(halves):
        for at, source in enumerate((down_a, down_b)):
            copies.append(
                pltpu.make_async_copy(
                    source.at[:, half], down_ref.at[pl.ds(at * units, units), half], sems.at[2 + 2 * n + at]
                )
            )
    for copy in copies:
        copy.start()
    merged = jnp.concatenate([piece[:, :depth] for piece in pieces], axis=0)
    hidden = []
    for at in range(2):
        copies[at].wait()
        value = lax.dot_general(
            merged, up_ref[at * units:(at + 1) * units, :], (((1,), (1,)), ((), ())),
            preferred_element_type=jnp.float32,
        )
        hidden.append((0.5 * value * (1.0 + lax.erf(value * (0.5 ** 0.5)))).astype(jnp.bfloat16))
    hidden = jnp.concatenate(hidden, axis=1)
    for n, half in enumerate(halves):
        copies[2 + 2 * n].wait()
        copies[3 + 2 * n].wait()
        for start in range(half.start, half.stop, CHUNK):
            total = jnp.dot(hidden, down_ref[:, start:start + CHUNK], preferred_element_type=jnp.float32)
            part = slice(start - half.start, start - half.start + CHUNK)
            if n == 0:
                for dx in range(X):
                    at = dx * Y * own
                    outs[dx][:, part] = total[at:at + Y * own].astype(outs[dx].dtype)
            else:
                for dx in range(X):
                    for dy in range(Y):
                        at = (dx * Y + dy) * own
                        outs[X + dy][dx * own:(dx + 1) * own, part] = total[at:at + own].astype(outs[X + dy].dtype)


def merger(pieces, ups, downs):
    units, depth = ups[0].shape
    width = downs[0].shape[1]
    own = pieces[0].shape[0] // Y
    shape = jax.ShapeDtypeStruct
    return pl.pallas_call(
        merger_kernel,
        in_specs=[VMEM] * X + [ANY] * 4,
        out_specs=[VMEM] * (X + Y),
        out_shape=[shape((Y * own, SUM_SPLIT), jnp.float32 if dx == 0 else jnp.bfloat16) for dx in range(X)]
        + [shape((X * own, width - SUM_SPLIT), jnp.float32 if dy == 0 else jnp.bfloat16) for dy in range(Y)],
        scratch_shapes=[
            pltpu.VMEM((2 * units, depth), jnp.bfloat16),
            pltpu.VMEM((2 * units, width), jnp.bfloat16),
            pltpu.SemaphoreType.DMA((6,)),
        ],
        compiler_params=pltpu.CompilerParams(vmem_limit_bytes=VMEM_BYTES),
        name="merger",
    )(*pieces, *ups, *downs)


def turned(part, cosine, sine):
    return part * cosine + pltpu.roll(part, HD // 2, 1) * sine


def slot_marks(b0, b1):
    cap = b0.shape[0] // Z
    at = b0.shape[1] - AUX
    blocks = []
    for dz in range(Z):
        for ref in (b0, b1):
            blocks.append(ref[dz * cap:(dz + 1) * cap, at:])
    return jnp.concatenate(blocks, axis=0), jnp.concatenate([b0[:, at:], b1[:, at:]], axis=0)


def slot_pick(marks, rows):
    value = marks.astype(jnp.float32)
    offset = value[:, 0:1] * 128.0 + value[:, 1:2]
    offset = jnp.where(value[:, 2:3] > 0.5, offset, -1.0).astype(jnp.int32)
    token = lax.broadcasted_iota(jnp.int32, (value.shape[0], rows), 1)
    return jnp.where(offset == token, 1.0, 0.0).T.astype(jnp.bfloat16)


def lane_sums(matrix):
    total = matrix[:, :HD]
    for at in range(HD, matrix.shape[1], HD):
        total += matrix[:, at:at + HD]
    return total


KV_BLOCK = 4


def slot_columns(refs, n, chunk):
    part = pl.ds(pl.multiple_of(n * chunk, chunk), chunk)
    return jnp.concatenate([ref[:, part] for ref in refs], axis=0)


def text_kernel(text_ref, weight_ref, kv_ref, total_ref):
    @pl.when(pl.program_id(0) == 0)
    def _():
        kv_ref[...] = jnp.zeros_like(kv_ref)
        total_ref[...] = jnp.zeros_like(total_ref)

    kv_ref[...] += jnp.dot(text_ref[...], weight_ref[...], preferred_element_type=jnp.float32)
    value = text_ref[...].astype(jnp.float32)
    total_ref[...] += lane_sums(value * value)


def project_text(text_rows, weights):
    rows, width = text_rows.shape
    kv_block = weights.shape[1] // (2 * HD) - 1
    shape = jax.ShapeDtypeStruct
    return pl.pallas_call(
        text_kernel,
        grid=(width // SLOT_CHUNK,),
        in_specs=[
            pl.BlockSpec((rows, SLOT_CHUNK), lambda n: (0, n)),
            pl.BlockSpec((SLOT_CHUNK, 2 * HD), lambda n: (n, kv_block)),
        ],
        out_specs=[whole((rows, 2 * HD)), whole((rows, HD))],
        out_shape=[shape((rows, 2 * HD), jnp.float32), shape((rows, HD), jnp.float32)],
        compiler_params=pltpu.CompilerParams(vmem_limit_bytes=VMEM_BYTES),
        name="project_text",
    )(text_rows, weights)


def slot_kernel(
    a0, a1, a2, a3, b0, b1, weight_ref, text_kv_ref, text_total_ref, cos_ref, sin_ref,
    kv_ref, scale_ref, sum_ref, total_ref,
):
    rows = text_kv_ref.shape[0]
    step = pl.program_id(0)
    steps = pl.num_programs(0)
    half = POOL_SPLIT // SLOT_CHUNK
    width = steps * SLOT_CHUNK

    @pl.when(step == 0)
    def _():
        sum_ref[...] = jnp.zeros_like(sum_ref)
        total_ref[...] = jnp.zeros_like(total_ref)

    def add(at, refs, index):
        slots = slot_columns(refs, index, SLOT_CHUNK)
        sum_ref[at] += jnp.dot(slots, weight_ref[...], preferred_element_type=jnp.float32)
        value = slots.astype(jnp.float32)
        total_ref[at] += lane_sums(value * value)

    @pl.when(step < half)
    def _():
        add(0, (a0, a1, a2, a3), step)

    @pl.when(step >= half)
    def _():
        add(1, (b0, b1), step - half)

    @pl.when(step == steps - 1)
    def _():
        marks = slot_marks(b0, b1)[1]
        pick = slot_pick(marks, rows)
        held = jnp.dot(pick, marks, preferred_element_type=jnp.float32)[:, 2:3] > 0.5
        cap = marks.shape[0] // (Z * YH)

        def joined(ref):
            first = [
                ref[0, (dz * YH + yh) * cap:(dz * YH + yh + 1) * cap, :] for yh in range(YH) for dz in range(Z)
            ]
            return jnp.concatenate(first, axis=0) + ref[1]

        def placed(value):
            high = value.astype(jnp.bfloat16)
            low = (value - high.astype(jnp.float32)).astype(jnp.bfloat16)
            return jnp.dot(pick, high, preferred_element_type=jnp.float32) + jnp.dot(
                pick, low, preferred_element_type=jnp.float32
            )

        def scale_of(total):
            return lax.rsqrt(jnp.sum(total, axis=1, keepdims=True) / width + NORM_EPS)

        slot_scale = scale_of(joined(total_ref))
        text_scale = scale_of(text_total_ref[...])
        slot_scale = jnp.broadcast_to(slot_scale, (slot_scale.shape[0], HD))
        scale = jnp.where(held, placed(slot_scale), text_scale)
        scale_ref[...] = scale
        kv = jnp.where(held, placed(joined(sum_ref)), text_kv_ref[...])
        kv_ref[:, :HD] = turned(kv[:, :HD] * scale, cos_ref[...], sin_ref[...]).astype(jnp.bfloat16)
        kv_ref[:, HD:] = (kv[:, HD:] * scale).astype(jnp.bfloat16)


def project_slots(slots_a, slots_b, weights, text_kv, text_total, cosine, sine):
    rows = text_kv.shape[0]
    width = weights.shape[0]
    slot_count = X * slots_a[0].shape[0]
    kv_block = weights.shape[1] // (2 * HD) - 1
    shape = jax.ShapeDtypeStruct
    return pl.pallas_call(
        slot_kernel,
        grid=(width // SLOT_CHUNK,),
        in_specs=[whole(piece.shape) for piece in slots_a]
        + [whole(piece.shape) for piece in slots_b]
        + [pl.BlockSpec((SLOT_CHUNK, 2 * HD), lambda n: (n, kv_block))]
        + [whole((rows, 2 * HD)), whole((rows, HD)), whole((rows, HD)), whole((rows, HD))],
        out_specs=[whole((rows, 2 * HD)), whole((rows, HD))],
        out_shape=[shape((rows, 2 * HD), jnp.bfloat16), shape((rows, HD), jnp.float32)],
        scratch_shapes=[
            pltpu.VMEM((2, slot_count, 2 * HD), jnp.float32),
            pltpu.VMEM((2, slot_count, HD), jnp.float32),
        ],
        compiler_params=pltpu.CompilerParams(vmem_limit_bytes=VMEM_BYTES),
        name="project_slots",
    )(*slots_a, *slots_b, weights, text_kv, text_total, cosine, sine)


GROUP = 2
SOFT = HD ** (-0.5) * LOG2E
LIMIT = 60.0


def query_kernel(
    text_ref, a0, a1, a2, a3, b0, b1, weight_ref, scale_ref, cos_ref, sin_ref, kv_ref, start_ref,
    q_ref, top_ref, sum_ref, acc_ref, pick_a, pick_b, held_ref, total_ref,
):
    rows = text_ref.shape[0]
    step = pl.program_id(0)
    steps = pl.num_programs(0)
    half = POOL_SPLIT // CHUNK
    wide = GROUP * rows

    @pl.when(step == 0)
    def _():
        marks_a, marks_b = slot_marks(b0, b1)
        pick_a[...] = slot_pick(marks_a, rows)
        pick_b[...] = slot_pick(marks_b, rows)
        held_ref[...] = jnp.dot(pick_b[...], marks_b, preferred_element_type=jnp.float32)
        total_ref[...] = jnp.zeros_like(total_ref)

    def add(pick, refs, index):
        slots = slot_columns(refs, index, CHUNK)
        image = jnp.dot(pick[...], slots, preferred_element_type=jnp.float32)
        mixed = jnp.where(held_ref[:, 2:3] > 0.5, image, text_ref[...].astype(jnp.float32)).astype(jnp.bfloat16)
        total_ref[...] += jnp.dot(mixed, weight_ref[...], preferred_element_type=jnp.float32)

    @pl.when(step < half)
    def _():
        add(pick_a, (a0, a1, a2, a3), step)

    @pl.when(step >= half)
    def _():
        add(pick_b, (b0, b1), step - half)

    @pl.when(step == steps - 1)
    def _():
        heads = total_ref.shape[1] // HD
        for h in range(heads):
            part = total_ref[:, h * HD:(h + 1) * HD] * scale_ref[...]
            q_ref[h * rows:(h + 1) * rows, :] = turned(part, cos_ref[...], sin_ref[...]).astype(jnp.bfloat16)
        key_at = lax.broadcasted_iota(jnp.int32, (rows, rows), 0)
        query_at = lax.broadcasted_iota(jnp.int32, (rows, rows), 1)
        allowed = (key_at <= query_at) & (key_at >= start_ref[0:1, :])
        allowed = jnp.concatenate([allowed] * GROUP, axis=1)
        for g in range(heads // GROUP):
            part = slice(g * wide, (g + 1) * wide)
            scores = lax.dot_general(
                kv_ref[:, :HD], q_ref[part, :], (((1,), (1,)), ((), ())), preferred_element_type=jnp.float32
            )
            scores = jnp.where(allowed, scores, BIG_NEG)
            top = jnp.max(scores, axis=0, keepdims=True)
            probs = jnp.exp2((scores - top) * SOFT)
            top_ref[:, part] = top
            sum_ref[:, part] = jnp.sum(probs, axis=0, keepdims=True)
            acc_ref[:, part] = lax.dot_general(
                kv_ref[:, HD:], probs.astype(jnp.bfloat16), (((0,), (0,)), ((), ())),
                preferred_element_type=jnp.float32,
            )


def query(text_rows, slots_a, slots_b, weights, scale, cosine, sine, kv, starts, heads):
    rows, width = text_rows.shape
    slot_count = X * slots_a[0].shape[0]
    wide = heads * rows
    shape = jax.ShapeDtypeStruct
    return pl.pallas_call(
        query_kernel,
        grid=(width // CHUNK,),
        in_specs=[pl.BlockSpec((rows, CHUNK), lambda n: (0, n))]
        + [whole(piece.shape) for piece in slots_a]
        + [whole(piece.shape) for piece in slots_b]
        + [pl.BlockSpec((CHUNK, heads * HD), lambda n: (n, 0))]
        + [whole((rows, HD))] * 3
        + [whole((rows, 2 * HD)), whole((1, rows))],
        out_specs=[whole((wide, HD)), whole((1, wide)), whole((1, wide)), whole((HD, wide))],
        out_shape=[
            shape((wide, HD), jnp.bfloat16),
            shape((1, wide), jnp.float32),
            shape((1, wide), jnp.float32),
            shape((HD, wide), jnp.float32),
        ],
        scratch_shapes=[
            pltpu.VMEM((rows, slot_count), jnp.bfloat16),
            pltpu.VMEM((rows, slot_count), jnp.bfloat16),
            pltpu.VMEM((rows, AUX), jnp.float32),
            pltpu.VMEM((rows, heads * HD), jnp.float32),
        ],
        compiler_params=pltpu.CompilerParams(vmem_limit_bytes=VMEM_BYTES),
        name="query",
    )(text_rows, *slots_a, *slots_b, weights, scale, cosine, sine, kv, starts)


def attention_kernel(
    info_ref, q_ref, top_in, sum_in, acc_in, kv_ref, start_ref, out_ref, base_ref, top_ref, sum_ref, acc_ref
):
    rows = out_ref.shape[0]
    heads = out_ref.shape[1] // HD
    wide = GROUP * rows
    me = info_ref[0]
    first = info_ref[1]
    clear = info_ref[2]
    count = me - first

    def allowed_keys(indices):
        masks = []
        for index in indices:
            key_at = (index - me) * rows + lax.broadcasted_iota(jnp.int32, (rows, rows), 0)
            masks.append(key_at >= start_ref[0:1, :])
        return jnp.concatenate([jnp.concatenate(masks, axis=0)] * GROUP, axis=1)

    def loaded(indices):
        keys = jnp.concatenate([kv_ref[index, :, :HD] for index in indices], axis=0)
        values = jnp.concatenate([kv_ref[index, :, HD:] for index in indices], axis=0)
        return keys, values

    def scores_of(keys, part, allowed):
        scores = lax.dot_general(
            keys, q_ref[part, :], (((1,), (1,)), ((), ())), preferred_element_type=jnp.float32
        )
        return scores if allowed is None else jnp.where(allowed, scores, BIG_NEG)

    def mixed_of(values, probs):
        return lax.dot_general(
            values, probs.astype(jnp.bfloat16), (((0,), (0,)), ((), ())), preferred_element_type=jnp.float32
        )

    def fast(indices, masked):
        keys, values = loaded(indices)
        allowed = allowed_keys(indices) if masked else None
        for g in range(heads // GROUP):
            part = slice(g * wide, (g + 1) * wide)
            scores = scores_of(keys, part, allowed)
            top_ref[:, part] = jnp.maximum(top_ref[:, part], jnp.max(scores, axis=0, keepdims=True))
            probs = jnp.exp2(scores * SOFT - base_ref[:, part])
            acc_ref[:, part] += mixed_of(values, probs)
            sum_ref[:, part] += jnp.sum(probs, axis=0, keepdims=True)

    def slow(index):
        keys, values = loaded([index])
        allowed = allowed_keys([index])
        for g in range(heads // GROUP):
            part = slice(g * wide, (g + 1) * wide)
            scores = scores_of(keys, part, allowed)
            old = top_ref[:, part]
            top = jnp.maximum(old, jnp.max(scores, axis=0, keepdims=True))
            probs = jnp.exp2((scores - top) * SOFT)
            shrink = jnp.exp2((old - top) * SOFT)
            top_ref[:, part] = top
            sum_ref[:, part] = sum_ref[:, part] * shrink + jnp.sum(probs, axis=0, keepdims=True)
            acc_ref[:, part] = acc_ref[:, part] * shrink + mixed_of(values, probs)

    def start():
        top_ref[...] = top_in[...]
        sum_ref[...] = sum_in[...]
        acc_ref[...] = acc_in[...]

    start()
    base_ref[...] = top_in[...] * SOFT
    def run(low, high, wide_step, masked):
        def several(i, _):
            at = high - 1 - wide_step * i
            fast([at - n for n in range(wide_step)], masked)
            return 0

        def single(i, _):
            fast([low + i], masked)
            return 0

        lax.fori_loop(0, (high - low) // wide_step, several, 0)
        lax.fori_loop(0, (high - low) % wide_step, single, 0)

    run(clear, me, 4, False)
    run(first, clear, 2, True)
    grown = jnp.max(top_ref[...] * SOFT - base_ref[...])

    @pl.when(grown > LIMIT)
    def _():
        start()

        def again(i, _):
            slow(me - 1 - i)
            return 0

        lax.fori_loop(0, count, again, 0)

    for h in range(heads):
        part = slice(h * rows, (h + 1) * rows)
        out_ref[:, h * HD:(h + 1) * HD] = (acc_ref[:, part] / sum_ref[:, part]).T.astype(jnp.bfloat16)


def attend(info, state, kv_all, starts):
    rows = kv_all.shape[1]
    wide = state[0].shape[0]
    vmem = pl.BlockSpec(memory_space=pltpu.VMEM)
    return pl.pallas_call(
        attention_kernel,
        in_specs=[pl.BlockSpec(memory_space=pltpu.SMEM)] + [vmem] * 6,
        out_specs=vmem,
        out_shape=jax.ShapeDtypeStruct((rows, wide // rows * HD), jnp.bfloat16),
        scratch_shapes=[
            pltpu.VMEM((1, wide), jnp.float32),
            pltpu.VMEM((1, wide), jnp.float32),
            pltpu.VMEM((1, wide), jnp.float32),
            pltpu.VMEM((HD, wide), jnp.float32),
        ],
        compiler_params=pltpu.CompilerParams(vmem_limit_bytes=VMEM_BYTES),
        name="attend",
    )(info, *state, kv_all, starts)


def per_device(
    patches,
    merge_up,
    merge_down,
    image_pos,
    text_rows,
    segment,
    query_weight,
    key_weight,
    value_weight,
):
    seq_count = lax.axis_size(SEQ)
    seq_index = lax.axis_index(SEQ)
    rows, width = text_rows.shape
    bf16, f32 = jnp.bfloat16, jnp.float32

    def after(array, *others):
        return lax.optimization_barrier((array, *others))[0]

    with jax.named_scope("merger"):
        merged = prepare(patches, segment)
        own = merged.shape[0]
        merged_beside = seq_shift(merged, 0, 1, 0)
        own_weights = jnp.concatenate(
            after((query_weight, key_weight, value_weight), merged_beside), axis=1
        )
        weights = lax.all_gather(own_weights, SEQ, axis=0, tiled=True)
        up_other = seq_shift(merge_up.T, 0, 0, 1)
        down_other = seq_shift(merge_down, 0, 0, 1)
        pair = jnp.concatenate([merged, merged_beside], axis=0)
        pieces = [pair] + [seq_shift(pair, dx, 0, 0) for dx in range(1, X)]
        outs = merger(pieces, (merge_up.T, up_other), (merge_down, down_other))
        part_a, part_b = outs[:X], outs[X:]

    with jax.named_scope("sums"):
        got_a = [seq_shift(part_a[dx], -dx, 0, 0) for dx in range(1, X)]
        got_b = seq_shift(part_b[1], 0, 1, 0)
        sum_a = part_a[0] + sum(piece.astype(f32) for piece in got_a)
        sum_b = part_b[0] + got_b.astype(f32)
        last_a = seq_shift(sum_a[own:].astype(bf16), 0, 1, 0)
        last_b = [seq_shift(sum_b[dx * own:(dx + 1) * own].astype(bf16), -dx, 0, 0) for dx in range(1, X)]
        image_a = (sum_a[:own] + last_a.astype(f32)).astype(bf16)
        image_b = (sum_b[:own] + sum(piece.astype(f32) for piece in last_b)).astype(bf16)

    with jax.named_scope("segments"):
        counted = sum(
            block[at:at + 1, merge_up.shape[0]:].astype(f32)
            for block in pieces
            for at in range(0, Y * own, own)
        )
        counted = (counted + seq_shift(counted, 0, 0, 1))[0]
        ends = (counted[:3] * 128.0 + counted[3:6]).astype(jnp.int32)
        before = jnp.concatenate([jnp.zeros((1,), jnp.int32), ends])
        starts = jnp.sum(
            jnp.where(segment[None, :] == jnp.arange(4, dtype=jnp.int32)[:, None], before[:, None], 0), axis=0
        )
        clear = jnp.minimum((starts[-1] + rows - 1) // rows, seq_index)
        info = jnp.stack([seq_index, starts[0] // rows, clear]).astype(jnp.int32)
        starts = (starts - seq_index * rows)[None, :]

    with jax.named_scope("angles"):
        positions = (seq_index * rows + jnp.arange(rows, dtype=jnp.int32)).astype(f32)
        frequency = ROPE_BASE ** (-(jnp.arange(HD // 2, dtype=f32) * 2.0 / HD))
        angles = positions[:, None] * frequency[None, :]
        cosine, sine = jnp.cos(angles), jnp.sin(angles)
        cosine = jnp.concatenate([cosine, cosine], axis=1)
        sine = jnp.concatenate([-sine, sine], axis=1)

    with jax.named_scope("route"):
        target = image_pos // rows
        offset = image_pos % rows
        matches = (target[:, None] == jnp.arange(seq_count, dtype=jnp.int32)[None, :]).astype(jnp.int32)
        slot_rank = jnp.sum((jnp.cumsum(matches, axis=0) - matches) * matches, axis=1)
        slot_index = target * CAP + slot_rank
        select = (slot_index[None, :] == jnp.arange(seq_count * CAP, dtype=jnp.int32)[:, None]).astype(bf16)
        marks = jnp.stack([offset // 128, offset % 128, jnp.ones_like(offset)], axis=1).astype(bf16)
        marks = jnp.pad(marks, ((0, 0), (0, AUX - 3)))
        send = jnp.dot(
            select, jnp.concatenate([image_a, image_b, marks], axis=1), preferred_element_type=f32
        ).astype(bf16)
        got = lax.all_to_all(
            send.reshape(seq_count, CAP, width + AUX), SEQ, split_axis=0, concat_axis=0, tiled=True
        ).reshape(seq_count * CAP, width + AUX)
        got, info, starts, cosine, sine = lax.optimization_barrier((got, info, starts, cosine, sine))
        got_a, got_b = got[:, :POOL_SPLIT], got[:, POOL_SPLIT:]
        pair_a = jnp.concatenate([got_a, pool_shift(got_a, 0, 1)], axis=0)
        column_b = jnp.concatenate([got_b] + [pool_shift(got_b, dz, 0) for dz in range(1, Z)], axis=0)
        pair_a, column_b, text_here = lax.optimization_barrier((pair_a, column_b, text_rows))
        slots_a = [pair_a] + [pool_shift(pair_a, dz, 0) for dz in range(1, Z)]
        slots_b = [column_b, pool_shift(column_b, 0, 1)]

    with jax.named_scope("project"):
        text_kv, text_total = project_text(text_here, weights)
        kv, scale = project_slots(slots_a, slots_b, weights, text_kv, text_total, cosine, sine)
        kv_all = lax.all_gather(kv, SEQ, axis=0, tiled=True)
        state = query(
            text_rows, slots_a, slots_b, weights, scale, cosine, sine, kv, starts, query_weight.shape[1] // HD
        )

    with jax.named_scope("attend"):
        return attend(info, state, kv_all.reshape(seq_count, rows, 2 * HD), starts)


def solution(mesh):
    return jax.shard_map(
        per_device,
        mesh=mesh,
        in_specs=(
            P(("pool", "seq"), None),
            P(None, "seq"),
            P("seq", None),
            P(("pool", "seq")),
            P("seq", None),
            P("seq"),
            P("seq", "pool"),
            P("seq", "pool"),
            P("seq", "pool"),
        ),
        out_specs=P("seq", "pool"),
        check_vma=False,
    )
```
